256 devices in a mesh: gx: 16 (over x, y), gy: 8 (over z), gz: 2 (over core).
Axes of the slice: x: 4, y: 4, z: 8, core: 2. Of those that a mesh axis runs over, the one named last changes fastest.
Arguments:
- fraction: float32 [32, 512, 1024], P('gz', 'gx', 'gy'), may hold values from 0 to 1
- velocity: float32 [3, 32, 512, 1024], P(None, 'gz', 'gx', 'gy'), may hold values from -0.45 to 0.45
- centres: int32 [3, 32768], P(None, ('gx', 'gy', 'gz')), may hold values from 3 to 130, as said below
- points: int32 [32768, 128], P(('gx', 'gy', 'gz')), may hold values from 0 to 342, as said below
- active_points: int32 [32768, 128], P(('gx', 'gy', 'gz')), may hold values 0 or 1
- counts: int32 [256], P(('gx', 'gy', 'gz')), may hold values from 1 to 128, as said below
- rigid_velocity_start: float32 [6, 32768], P(None, ('gx', 'gy', 'gz')), may hold values from -1.5 to 1.5
- inverse_mass: float32 [32768], P(('gx', 'gy', 'gz')), may hold values from 0.004 to 0.012
- inverse_inertia: float32 [32768], P(('gx', 'gy', 'gz')), may hold values from 0.01 to 0.03
Outputs:
- fraction_out: float32 [32, 512, 1024], P('gz', 'gx', 'gy')
- curvature: float32 [512, 1024], P('gx', 'gy')
- multipliers: float32 [3, 32768, 128], P(None, ('gx', 'gy', 'gz'))
- rigid_motion: float32 [6, 32768], P(None, ('gx', 'gy', 'gz'))
The draws below stay inside these ranges and needn't reach their ends.
Inputs may be any that keep to these rules, and one draw needn't show every extreme that they name: `centres`: each component lies inside the slot's own brick in the widened block: 3 to 18 vertically, to 34 streamwise, to 130 spanwise. `points`: each code names a displacement of at most 3 cells along each direction. `counts`: bricks with even numbers (lower vertical half) own 128 // 2 to 128 particles, those with odd numbers 1 to 64.
All inputs are finite; a program needn't handle non-finite values. No bound on the sum of `active_points` on one device may be relied on, other than what follows from the above.
Results may differ from the reference program's by a relative error of at most 0.00014.
Values sent between devices are 32-bit elements; how exact they have to be, the bound alone decides.
A program may use at most 192 MiB of HBM per device.

```python
import math
import jax
import jax.numpy as jnp
from jax import lax

CZ = 16
CX = 32
CY = 128
P_DEV = 128
PARTICLE_POINTS = 128
POINT_REACH = 3
UZAWA = 2
NZ = 32
NX = 512
NY = 1024
BRICKS = 256
SLOT_TOTAL = 32768
N_GY = 8
N_GZ = 2


def particle_layout(key):
    base_key = jax.random.fold_in(key, 11)
    split_keys = jax.random.split(base_key, 4)
    lower_bounds = jnp.array([POINT_REACH, POINT_REACH, POINT_REACH], jnp.int32)
    upper_bounds = jnp.array([CZ + POINT_REACH, CX + POINT_REACH, CY + POINT_REACH], jnp.int32)
    centres = jax.random.randint(split_keys[0], (3, SLOT_TOTAL), lower_bounds[:, None], upper_bounds[:, None])
    highest_slot = jax.random.randint(split_keys[1], (), 0, SLOT_TOTAL)
    bottom_slot = (highest_slot + 1 + jax.random.randint(split_keys[2], (), 0, SLOT_TOTAL - 1)) % SLOT_TOTAL
    slot_number_index = jnp.arange(SLOT_TOTAL, dtype=jnp.int32)
    centres = jnp.where(slot_number_index[None] == highest_slot, upper_bounds[:, None] - 1, centres)
    centres = jnp.where(slot_number_index[None] == bottom_slot, lower_bounds[:, None], centres)
    cell_shifts = jax.random.randint(split_keys[3], (3, SLOT_TOTAL, PARTICLE_POINTS), -POINT_REACH, POINT_REACH + 1)
    first_point = jnp.arange(PARTICLE_POINTS, dtype=jnp.int32)[None, :] == 0
    cell_shifts = jnp.where((slot_number_index[:, None] == highest_slot) & first_point, POINT_REACH, cell_shifts)
    cell_shifts = jnp.where((slot_number_index[:, None] == bottom_slot) & first_point, -POINT_REACH, cell_shifts)
    shift_span = 2 * POINT_REACH + 1
    codes = ((cell_shifts[0] + POINT_REACH) * shift_span + cell_shifts[1] + POINT_REACH) * shift_span + cell_shifts[2] + POINT_REACH
    return (centres, codes)


def draw_centres(key, part):
    return particle_layout(key)[0]


def draw_points(key, part):
    return particle_layout(key)[1]


def draw_counts(key, part):
    split_keys = jax.random.split(jax.random.fold_in(key, 23), 4)
    brick_index = jnp.arange(BRICKS, dtype=jnp.int32)
    lower_half = brick_index % 2 == 0
    heavy_load = jax.random.randint(split_keys[0], (BRICKS,), P_DEV // 2, P_DEV + 1)
    light_load = jax.random.randint(split_keys[1], (BRICKS,), 1, P_DEV // 2 + 1)
    loads = jnp.where(lower_half, heavy_load, light_load)
    full_brick = 2 * jax.random.randint(split_keys[2], (), 0, BRICKS // 2)
    single_brick = 2 * jax.random.randint(split_keys[3], (), 0, BRICKS // 2) + 1
    loads = jnp.where(brick_index == full_brick, P_DEV, loads)
    return jnp.where(brick_index == single_brick, 1, loads)


def with_ends(drawn, stream_key, least, largest):
    longest = drawn.shape.index(max(drawn.shape))
    spots = []
    for shift in (0, 1):
        where = [jax.random.randint(jax.random.fold_in(stream_key, axis), (), 0, length) for axis, length in enumerate(drawn.shape)]
        where[longest] = (where[longest] + shift) % drawn.shape[longest]
        spots.append(tuple(where))
    return drawn.at[spots[0]].set(least).at[spots[1]].set(largest)


def block_levels(rng, dims, cuts, smallest, top_value):
    def one(dim, parts):
        draws = jax.random.uniform(jax.random.fold_in(jax.random.fold_in(rng, 6), dim), (parts,), jnp.float32, smallest / len(cuts), top_value / len(cuts))
        return jnp.repeat(jnp.exp(draws), dims[dim] // parts).reshape((-1,) + (1,) * (len(dims) - dim - 1))

    loudness = one(*cuts[0])
    for cut in cuts[1:]:
        loudness = loudness * one(*cut)
    return loudness


def noise(rng, shape, spread, limit, cuts=(), held_as=jnp.bfloat16):
    loudness = block_levels(rng, shape, cuts, -0.22, 0.18) if cuts else 1.0
    values = jax.random.normal(rng, shape, jnp.float32) * spread * loudness
    return jnp.minimum(jnp.maximum(values, -limit), limit).astype(held_as)


def setup_inputs(seed: int = 0) -> dict:
    streams_of = jax.random.split(jax.random.key(seed), 10)
    return {
        "fraction": jnp.clip(1.0 * jax.random.uniform(streams_of[0], (NZ, NX, NY), jnp.float32) ** block_levels(streams_of[0], (NZ, NX, NY), ((0, 2), (1, 16), (2, 8)), -0.2, 0.2), 0.0, 1.0),
        "velocity": jnp.clip(jax.random.uniform(streams_of[1], (3, NZ, NX, NY), jnp.float32, -0.45, 0.45) * block_levels(streams_of[1], (3, NZ, NX, NY), ((1, 2), (2, 16), (3, 8)), -0.4, 0.0), -0.45, 0.45),
        "centres": draw_centres(jax.random.fold_in(streams_of[9], 71), 0),
        "points": draw_points(jax.random.fold_in(streams_of[9], 71), 0),
        "active_points": with_ends((jax.random.randint(streams_of[4], (SLOT_TOTAL, PARTICLE_POINTS), 0, 4) < 3).astype(jnp.int32), jax.random.fold_in(streams_of[4], 1), 0, 1),
        "counts": draw_counts(jax.random.fold_in(streams_of[9], 71), 0),
        "rigid_velocity_start": noise(streams_of[6], (6, SLOT_TOTAL), 0.3, 1.5, ((1, 256),), jnp.float32),
        "inverse_mass": jnp.clip(jnp.exp(math.log(0.012) - 1.09861225 * jax.random.uniform(streams_of[7], (SLOT_TOTAL,), jnp.float32) ** block_levels(streams_of[7], (SLOT_TOTAL,), ((0, 256),), -0.2, 0.2)), 0.004, 0.012),
        "inverse_inertia": jnp.clip(jnp.exp(math.log(0.03) - 1.0986123 * jax.random.uniform(streams_of[8], (SLOT_TOTAL,), jnp.float32) ** block_levels(streams_of[8], (SLOT_TOTAL,), ((0, 256),), -0.2, 0.2)), 0.01, 0.03),
    }


RHO_STEP = 1.0
BETA_FLUID = 0.5

def sweep_front(frac_pad, speed_pad):
    face_speed = 0.5 * (speed_pad[:-1] + speed_pad[1:])
    face_flux = jnp.maximum(face_speed, 0.0) * frac_pad[:-1] + jnp.minimum(face_speed, 0.0) * frac_pad[1:]
    interior = frac_pad[1:-1]
    return interior - (face_flux[1:] - face_flux[:-1]) + interior * (face_speed[1:] - face_speed[:-1])

def sweep_along(frac_pad, speed_pad, along_axis):
    result = sweep_front(jnp.moveaxis(frac_pad, along_axis, 0), jnp.moveaxis(speed_pad, along_axis, 0))
    return jnp.moveaxis(result, 0, along_axis)

def pad_along(values_in, along_axis):
    widths = [(0, 0)] * values_in.ndim
    widths[along_axis] = (1, 1)
    return jnp.pad(values_in, widths)

def curvature_of(height_pad):
    middle = height_pad[1:-1, 1:-1]
    east_side = height_pad[2:, 1:-1]
    west_side = height_pad[:-2, 1:-1]
    north_side = height_pad[1:-1, 2:]
    south_side = height_pad[1:-1, :-2]
    slope_x = 0.5 * (east_side - west_side)
    slope_y = 0.5 * (north_side - south_side)
    bend_xx = east_side - 2.0 * middle + west_side
    bend_yy = north_side - 2.0 * middle + south_side
    bend_xy = 0.25 * (height_pad[2:, 2:] - height_pad[2:, :-2] - height_pad[:-2, 2:] + height_pad[:-2, :-2])
    metric = 1.0 + slope_x * slope_x + slope_y * slope_y
    top_part = bend_xx * (1.0 + slope_y * slope_y) + bend_yy * (1.0 + slope_x * slope_x) - 2.0 * slope_x * slope_y * bend_xy
    return top_part / (metric * jnp.sqrt(metric))

def cross_of(former, latter):
    return jnp.stack([former[1] * latter[2] - former[2] * latter[1], former[2] * latter[0] - former[0] * latter[2], former[0] * latter[1] - former[1] * latter[0]])

def uzawa_steps(sampled, offsets, weight, rigid_velocity_start, inverse_mass, inverse_inertia, alive_mask):
    multipliers = jnp.zeros_like(sampled)
    linear_start = rigid_velocity_start[:3]
    angular_start = rigid_velocity_start[3:]
    linear = linear_start
    angular = angular_start
    for iteration in range(UZAWA):
        moving = linear[:, :, None] + cross_of(angular[:, :, None], offsets)
        multipliers = (multipliers + RHO_STEP * (sampled - BETA_FLUID * multipliers - moving)) * weight[None]
        net_force = lax.optimization_barrier(jnp.sum(multipliers, axis=2))
        torque = lax.optimization_barrier(jnp.sum(cross_of(offsets, multipliers), axis=2))
        linear = linear_start + inverse_mass[None] * net_force
        angular = angular_start + inverse_inertia[None] * torque
    rigid_motion = jnp.concatenate([linear, angular], axis=0) * alive_mask[None]
    return (multipliers, rigid_motion)

def reference(fraction, velocity, centres, points, active_points, counts, rigid_velocity_start, inverse_mass, inverse_inertia):
    current = fraction
    for along_axis in (1, 2, 0):
        current = sweep_along(pad_along(current, along_axis), pad_along(velocity[along_axis], along_axis), along_axis)
    heights = lax.optimization_barrier(jnp.sum(current, axis=0))
    curvature = curvature_of(jnp.pad(heights, 1))
    padded = jnp.pad(velocity, ((0, 0), (POINT_REACH, POINT_REACH), (POINT_REACH, POINT_REACH), (POINT_REACH, POINT_REACH)))
    shift_span = 2 * POINT_REACH + 1
    slot_number_index = jnp.arange(SLOT_TOTAL, dtype=jnp.int32)
    slot_brick = slot_number_index // P_DEV
    brick_x = slot_brick // (N_GY * N_GZ)
    brick_y = slot_brick // N_GZ % N_GY
    brick_z = slot_brick % N_GZ
    shift_depth = points // (shift_span * shift_span) - POINT_REACH
    shift_row = points // shift_span % shift_span - POINT_REACH
    shift_col = points % shift_span - POINT_REACH
    cell_depth = centres[0][:, None] + shift_depth
    cell_row = centres[1][:, None] + shift_row
    cell_col = centres[2][:, None] + shift_col
    sampled = padded[:, cell_depth + (brick_z * CZ)[:, None], cell_row + (brick_x * CX)[:, None], cell_col + (brick_y * CY)[:, None]]
    offsets = jnp.stack([shift_depth, shift_row, shift_col]).astype(jnp.float32)
    alive_mask = (slot_number_index % P_DEV < counts[slot_brick]).astype(jnp.float32)
    weight = active_points.astype(jnp.float32) * alive_mask[:, None]
    multipliers, rigid_motion = uzawa_steps(sampled, offsets, weight, rigid_velocity_start, inverse_mass, inverse_inertia, alive_mask)
    return (current, curvature, multipliers, rigid_motion)
```

```python
import jax
import jax.numpy as jnp
from jax import lax
from jax.experimental import pallas as pl
from jax.experimental.pallas import tpu as pltpu
from jax.sharding import PartitionSpec as P

MESH = pl.DeviceIdType.MESH
F32 = jnp.float32
I32 = jnp.int32

ACROSS = [(dx, dy) for dx in (-1, 0, 1) for dy in (-1, 0, 1) if dx or dy]


def lanes_of(shape):
    return lax.broadcasted_iota(I32, shape, len(shape) - 1)


def turn(x, by):
    by %= 128
    return pltpu.roll(x, by, x.ndim - 1) if by else x


def halo_kernel(
    frac, vel, T, fout, curv,
    F, QU, QD, RQL, RQH, PL, PR, RL, RR, RZ, RZF, SQ, HB, HP, HX, HY, HC, HS, HN, HM,
    in_sem, send, recv, hsend, hrecv,
):
    gx, gy, gz = (lax.axis_index(a) for a in ("gx", "gy", "gz"))

    def place(dx, dy, dz):
        return (lax.rem(gx + dx + 16, 16), lax.rem(gy + dy + 8, 8), gz if dz == 0 else 1 - gz)

    everyone = [(dx, dy, dz) for dz in (0, 1) for dx, dy in ACROSS] + [(0, 0, 1)]
    own = []
    for side in (0, 1):
        own.append(pltpu.make_async_copy(vel, T.at[side, :, 4:20, 8:40, :], in_sem.at[2 * side]))
        own.append(pltpu.make_async_copy(frac, F.at[side, 4:20, 8:40, :], in_sem.at[2 * side + 1]))
    for c in own:
        c.start()

    barrier = pltpu.get_barrier_semaphore()
    for off in everyone:
        pl.semaphore_signal(barrier, inc=1, device_id=place(*off), device_id_type=MESH)
    pl.semaphore_wait(barrier, len(everyone))

    low = 12 * (1 - gz)
    copies = {}
    count = [0]

    def start(key, src, dst, off):
        k = count[0]
        count[0] += 1
        c = pltpu.make_async_remote_copy(
            src_ref=src, dst_ref=dst, send_sem=send.at[k], recv_sem=recv.at[k], device_id=place(*off),
            device_id_type=MESH,
        )
        c.start()
        copies[key] = c

    start("z", vel.at[:, pl.ds(low, 4)], RZ, (0, 0, 1))
    start("zf", frac.at[pl.ds(low, 4)], RZF, (0, 0, 1))
    for c in own:
        c.wait()

    def pack_rows(g, _):
        for dd in range(4):
            for c in range(3):
                at = 10 * dd + 3 * c
                QU[g, at : at + 3, :] = T[1, c, 4 + 4 * g + dd, 37:40, :]
                QD[g, at : at + 3, :] = T[1, c, 4 + 4 * g + dd, 8:11, :]
            at = 10 * dd + 9
            QU[g, at : at + 1, :] = F[1, 4 + 4 * g + dd, 39:40, :]
            QD[g, at : at + 1, :] = F[1, 4 + 4 * g + dd, 8:9, :]
        return 0

    lax.fori_loop(0, 4, pack_rows, 0)
    for dx, src, dst in ((1, QU, RQL), (-1, QD, RQH)):
        start((dx, 0, 0), src, dst.at[1:5], (dx, 0, 0))
        start((dx, 0, 1), src.at[3 * (1 - gz)], dst.at[5 * gz], (dx, 0, 1))

    lane = lanes_of((8, 128))
    spot = lane // 8
    first = (lane % 8) < 4

    def pack_lanes(t, _):
        rows = pl.ds(pl.multiple_of(8 + 8 * t, 8), 8)
        both = []
        for g in range(4):
            acc = None
            for i in range(16):
                c, d = i // 4, 4 + 4 * g + i % 4
                v = turn(T[1, c, d, rows, :] if c < 3 else F[1, d, rows, :], 8 * i + 4)
                acc = v if i == 0 else jnp.where(spot == i, v, acc)
            both.append(acc)
        for h in range(2):
            a, b = both[2 * h], both[2 * h + 1]
            PL[h, t] = jnp.where(first, a, turn(b, 4))
            PR[h, t] = jnp.where(first, turn(a, -4), b)
        return 0

    lax.fori_loop(0, 4, pack_lanes, 0)
    for dy, src, dst in ((1, PL, RL), (-1, PR, RR)):
        for dx in (0, 1, -1):
            ts, td = {0: (slice(0, 4), slice(1, 5)), 1: (3, 0), -1: (0, 5)}[dx]
            start((dx, dy, 0), src.at[:, ts], dst.at[1:3, td], (dx, dy, 0))
            start((dx, dy, 1), src.at[1 - gz, ts], dst.at[3 * gz, td], (dx, dy, 1))

    RQL[5 * gz] = jnp.zeros((40, 128), F32)
    RQH[5 * gz] = jnp.zeros((40, 128), F32)
    RL[3 * gz] = jnp.zeros((6, 8, 128), F32)
    RR[3 * gz] = jnp.zeros((6, 8, 128), F32)
    blank = jnp.zeros((4, 32, 128), F32)
    for side in (0, 1):
        for c in range(3):
            T[side, c, pl.ds(20 * gz, 4), 8:40, :] = blank
        F[side, pl.ds(20 * gz, 4), 8:40, :] = blank
    copies["z"].wait()
    copies["zf"].wait()
    for side in (0, 1):
        for c in range(3):
            T[side, c, pl.ds(20 * (1 - gz), 4), 8:40, :] = RZ[c]
        F[side, pl.ds(20 * (1 - gz), 4), 8:40, :] = RZF[...]

    in_low, in_high = (gx > 0).astype(F32), (gx < 15).astype(F32)
    in_left, in_right = (gy > 0).astype(F32), (gy < 7).astype(F32)
    for dx, src, to, here in ((1, RQL, 5, in_low), (-1, RQH, 40, in_high)):
        copies[(dx, 0, 0)].wait()
        copies[(dx, 0, 1)].wait()

        def unpack_rows(g, _):
            for dd in range(4):
                for c in range(3):
                    at = 10 * dd + 3 * c
                    v = src[g, at : at + 3, :] * here
                    T[0, c, 4 * g + dd, to : to + 3, :] = v
                    T[1, c, 4 * g + dd, to : to + 3, :] = v
                at = 10 * dd + 9
                v = src[g, at : at + 1, :] * here
                one = 7 if to == 5 else 40
                F[0, 4 * g + dd, one : one + 1, :] = v
                F[1, 4 * g + dd, one : one + 1, :] = v
            return 0

        lax.fori_loop(0, 6, unpack_rows, 0)

    for dy in (1, -1):
        for dx in (0, 1, -1):
            copies[(dx, dy, 0)].wait()
            copies[(dx, dy, 1)].wait()

    outer_left, outer_right = lane >= 96, lane < 32

    def unpack_lanes(t, _):
        rows = pl.ds(pl.multiple_of(8 * t, 8), 8)
        here = jnp.where(t == 0, in_low, jnp.where(t == 5, in_high, 1.0))
        left, right = in_left * here, in_right * here
        for s in range(4):
            a, b = RL[s, t] * left, RR[s, t] * right
            for part in (0, 1):
                g = 2 * s - 1 + part
                if g < 0 or g > 5:
                    continue
                v = jnp.where(first, a, turn(b, 4)) if part == 0 else jnp.where(first, turn(a, -4), b)
                for i in range(16):
                    c, d = i // 4, 4 * g + i % 4
                    if d in (0, 23):
                        continue
                    w = turn(v, 124 - 8 * i)
                    if c < 3:
                        T[0, c, d, rows, :] = jnp.where(outer_left, w, T[0, c, d, rows, :])
                        T[1, c, d, rows, :] = jnp.where(outer_right, w, T[1, c, d, rows, :])
                    else:
                        F[0, d, rows, :] = jnp.where(outer_left, w, F[0, d, rows, :])
                        F[1, d, rows, :] = jnp.where(outer_right, w, F[1, d, rows, :])
        return 0

    lax.fori_loop(0, 6, unpack_lanes, 0)

    wide = lanes_of((32, 128))
    right_half = wide >= 64
    head, tail = wide == 0, wide == 127

    def flux_of(speed, below, above):
        return jnp.maximum(speed, 0.0) * below + jnp.minimum(speed, 0.0) * above

    def swept(q, flux_low, flux_high, speed_low, speed_high):
        return q - (flux_high - flux_low) + q * (speed_high - speed_low)

    def two(read):
        a, b = read(0), read(1)
        return jnp.where(right_half, b, a), jnp.where(right_half, a, b)

    def sweep_xy(k, _):
        d = 3 + k
        q3 = [two(lambda s, o=o: F[s, d, 7 + o : 39 + o, :]) for o in range(3)]
        u3 = [two(lambda s, o=o: T[s, 1, d, 7 + o : 39 + o, :]) for o in range(3)]
        done = []
        for which in (0, 1):
            q, u = [x[which] for x in q3], [x[which] for x in u3]
            lo, hi = 0.5 * (u[0] + u[1]), 0.5 * (u[1] + u[2])
            done.append(swept(q[1], flux_of(lo, q[0], q[1]), flux_of(hi, q[1], q[2]), lo, hi))
        q, qh = done
        u, uh = two(lambda s: T[s, 2, d, 8:40, :])
        ql, ul = turn(jnp.where(tail, qh, q), 1), turn(jnp.where(tail, uh, u), 1)
        qr, ur = turn(jnp.where(head, qh, q), -1), turn(jnp.where(head, uh, u), -1)
        lo, hi = 0.5 * (ul + u), 0.5 * (u + ur)
        SQ[k] = swept(q, flux_of(lo, ql, q), flux_of(hi, q, qr), lo, hi)
        return 0

    lax.fori_loop(0, 18, sweep_xy, 0)

    HB[...] = jnp.zeros((32, 128), F32)

    def sweep_z(k, _):
        q = [SQ[k + o] for o in range(3)]
        u = [two(lambda s, o=o: T[s, 0, 3 + k + o, 8:40, :])[0] for o in range(3)]
        lo, hi = 0.5 * (u[0] + u[1]), 0.5 * (u[1] + u[2])
        new = swept(q[1], flux_of(lo, q[0], q[1]), flux_of(hi, q[1], q[2]), lo, hi)
        fout[k] = new
        HB[...] += new
        return 0

    lax.fori_loop(0, 16, sweep_z, 0)

    heights = []
    for j, (dx, dy, dz) in enumerate(everyone):
        rows = {0: slice(0, 32), 1: slice(24, 32), -1: slice(0, 8)}[dx]
        if dx == 0 and dy == 0:
            dst = HP
        elif dy == 0:
            dst = HX.at[dz, (dx < 0) * 1]
        elif dx == 0:
            dst = HY.at[dz, (dy < 0) * 1]
        else:
            dst = HC.at[dz, (dx < 0) * 2 + (dy < 0) * 1]
        c = pltpu.make_async_remote_copy(
            src_ref=HB.at[rows], dst_ref=dst, send_sem=hsend.at[j], recv_sem=hrecv.at[j],
            device_id=place(dx, dy, dz), device_id_type=MESH,
        )
        c.start()
        heights.append(c)
    for c in heights:
        c.wait()

    HS[0, 8:40] = HB[...] + HP[...]
    HS[0, 0:8] = (HX[0, 0] + HX[1, 0]) * in_low
    HS[0, 40:48] = (HX[0, 1] + HX[1, 1]) * in_high
    HS[1, 8:40] = jnp.where(
        right_half, (HY[0, 0] + HY[1, 0]) * in_left, (HY[0, 1] + HY[1, 1]) * in_right
    )
    for x, at, here in ((0, 0, in_low), (1, 40, in_high)):
        HS[1, at : at + 8] = jnp.where(
            lane >= 64,
            (HC[0, 2 * x] + HC[1, 2 * x]) * (in_left * here),
            (HC[0, 2 * x + 1] + HC[1, 2 * x + 1]) * (in_right * here),
        )
    all_lanes = lanes_of((48, 128))
    h, hh = HS[0], HS[1]
    HN[...] = turn(jnp.where(all_lanes == 0, hh, h), -1)
    HM[...] = turn(jnp.where(all_lanes == 127, hh, h), 1)
    middle, east, west = HS[0, 8:40], HS[0, 9:41], HS[0, 7:39]
    north, south = HN[8:40], HM[8:40]
    slope_x, slope_y = 0.5 * (east - west), 0.5 * (north - south)
    bend_xx = east - 2.0 * middle + west
    bend_yy = north - 2.0 * middle + south
    bend_xy = 0.25 * (HN[9:41] - HM[9:41] - HN[7:39] + HM[7:39])
    metric = 1.0 + slope_x * slope_x + slope_y * slope_y
    top = (
        bend_xx * (1.0 + slope_y * slope_y) + bend_yy * (1.0 + slope_x * slope_x)
        - 2.0 * slope_x * slope_y * bend_xy
    )
    curv[...] = top / (metric * jnp.sqrt(metric))


def along(x, idx, axis):
    return jnp.take_along_axis(x, idx, axis=axis, mode="promise_in_bounds")


GROUP = 16


def particle_kernel(
    cen, counts, T, fin, cin, points, active, start, mass, inertia,
    fout, cout, mult, motion, ED, ER, EC, A, AT, RM, sem,
):
    passed = [pltpu.make_async_copy(fin, fout, sem.at[0]), pltpu.make_async_copy(cin, cout, sem.at[1])]
    for c in passed:
        c.start()
    code = points[...]
    ed = (code * 1338) >> 16
    rest = code - ed * 49
    er = (rest * 9363) >> 16
    ED[...] = ed
    ER[...] = er
    EC[...] = rest - er * 7
    A[...] = jnp.zeros((128, 128), F32)
    A[0:6, :] = start[...]
    A[6:7, :] = mass[...]
    A[7:8, :] = inertia[...]
    AT[...] = A[...].T
    owned = counts[0]
    lane = lanes_of((GROUP, 128))
    row8 = lax.broadcasted_iota(I32, (8, 128), 0)

    def cross(a, b):
        return [a[1] * b[2] - a[2] * b[1], a[2] * b[0] - a[0] * b[2], a[0] * b[1] - a[1] * b[0]]

    def group(g, _):
        base = pl.multiple_of(g * GROUP, GROUP)
        tiles = [[None] * (GROUP // 8) for _ in range(3)]
        for s in range(GROUP):
            q = base + s
            d0 = cen[0, q] - 2
            r0 = cen[1, q] + 2
            jc = cen[2, q] - 3
            side = (jc >= 64).astype(I32)
            e_d = jnp.broadcast_to(ED[pl.ds(q, 1), :], (8, 128))
            e_r = jnp.broadcast_to(ER[pl.ds(q, 1), :], (8, 128))
            idx = (jnp.broadcast_to(EC[pl.ds(q, 1), :], (8, 128)) + (jc - 3)) & 127
            picks = [e_d == k for k in range(1, 7)]
            for c in range(3):
                acc = None
                for k in range(7):
                    v = along(T[side, c, d0 + k, pl.ds(r0, 8), :], idx, 1)
                    acc = v if k == 0 else jnp.where(picks[k - 1], v, acc)
                res = along(acc, e_r, 0)
                old = tiles[c][s // 8]
                tiles[c][s // 8] = res if s % 8 == 0 else jnp.where(row8 == s % 8, res, old)
        sampled = [jnp.concatenate(t, axis=0) for t in tiles]
        rows = pl.ds(base, GROUP)
        offsets = [(e[rows, :] - 3).astype(F32) for e in (ED, ER, EC)]
        alive = ((lax.broadcasted_iota(I32, (GROUP, 128), 0) + base) < owned).astype(F32)
        weight = active[rows, :].astype(F32) * alive
        columns = AT[rows, :]
        column = [columns[:, k : k + 1] for k in range(8)]
        linear, angular = column[0:3], column[3:6]
        m = None
        for it in range(2):
            spin = cross(angular, offsets)
            moving = [linear[k] + spin[k] for k in range(3)]
            if it == 0:
                m = [(sampled[k] - moving[k]) * weight for k in range(3)]
            else:
                m = [(m[k] + (sampled[k] - 0.5 * m[k] - moving[k])) * weight for k in range(3)]
            torque = cross(offsets, m)
            linear = [column[k] + column[6] * jnp.sum(m[k], axis=1, keepdims=True) for k in range(3)]
            angular = [column[3 + k] + column[7] * jnp.sum(torque[k], axis=1, keepdims=True) for k in range(3)]
        for k in range(3):
            mult[k, rows, :] = m[k]
        out = jnp.zeros((GROUP, 128), F32)
        for k in range(6):
            out = jnp.where(lane == k, (linear + angular)[k], out)
        RM[rows, :] = out * alive
        return 0

    lax.fori_loop(0, 128 // GROUP, group, 0)
    motion[...] = RM[...].T[0:6, :]
    for c in passed:
        c.wait()


def body(fraction, velocity, centres, points, active_points, counts, rigid_start, mass, inertia):
    vmem, smem = pl.BlockSpec(memory_space=pltpu.VMEM), pl.BlockSpec(memory_space=pltpu.SMEM)
    anywhere = pl.BlockSpec(memory_space=pl.ANY)

    def f32(*shape):
        return jax.ShapeDtypeStruct(shape, F32)

    def room(*shape):
        return pltpu.VMEM(shape, F32)

    table, swept, curvature = pl.pallas_call(
        halo_kernel,
        out_shape=(f32(2, 3, 24, 48, 128), f32(16, 32, 128), f32(32, 128)),
        in_specs=[anywhere] * 2,
        out_specs=(vmem, vmem, vmem),
        scratch_shapes=[
            room(2, 24, 48, 128),
            room(4, 40, 128), room(4, 40, 128), room(6, 40, 128), room(6, 40, 128),
            room(2, 4, 8, 128), room(2, 4, 8, 128), room(4, 6, 8, 128), room(4, 6, 8, 128),
            room(3, 4, 32, 128), room(4, 32, 128), room(18, 32, 128),
            room(32, 128), room(32, 128), room(2, 2, 8, 128), room(2, 2, 32, 128), room(2, 4, 8, 128),
            room(2, 48, 128), room(48, 128), room(48, 128),
            pltpu.SemaphoreType.DMA((4,)),
            pltpu.SemaphoreType.DMA((18,)), pltpu.SemaphoreType.DMA((18,)),
            pltpu.SemaphoreType.DMA((17,)), pltpu.SemaphoreType.DMA((17,)),
        ],
        compiler_params=pltpu.CompilerParams(
            collective_id=0, has_side_effects=True, vmem_limit_bytes=40 << 20
        ),
        name="halo_and_sweeps",
    )(fraction, velocity)
    return pl.pallas_call(
        particle_kernel,
        out_shape=(f32(16, 32, 128), f32(32, 128), f32(3, 128, 128), f32(6, 128)),
        in_specs=[smem, smem, vmem, anywhere, anywhere] + [vmem] * 5,
        out_specs=(anywhere, anywhere, vmem, vmem),
        scratch_shapes=[pltpu.VMEM((128, 128), I32)] * 3 + [room(128, 128)] * 3 + [pltpu.SemaphoreType.DMA((2,))],
        compiler_params=pltpu.CompilerParams(vmem_limit_bytes=40 << 20),
        name="particles",
    )(
        centres, counts, table, swept, curvature, points, active_points, rigid_start,
        mass.reshape(1, 128), inertia.reshape(1, 128),
    )


def solution(mesh):
    bricks = ("gx", "gy", "gz")
    placed = (
        P("gz", "gx", "gy"), P(None, "gz", "gx", "gy"), P(None, bricks), P(bricks, None), P(bricks, None),
        P(bricks), P(None, bricks), P(bricks), P(bricks),
    )
    return jax.shard_map(
        body, mesh=mesh, in_specs=placed,
        out_specs=(P("gz", "gx", "gy"), P("gx", "gy"), P(None, bricks, None), P(None, bricks)),
        check_vma=False,
    )
```

```python
import jax
import jax.numpy as jnp
from jax import lax
from jax.experimental import pallas as pl
from jax.experimental.pallas import tpu as pltpu
from jax.sharding import PartitionSpec as P

MESH = pl.DeviceIdType.MESH
GROUP = 16
F32 = jnp.float32
I32 = jnp.int32

ACROSS = [(dx, dy) for dx in (-1, 0, 1) for dy in (-1, 0, 1) if dx or dy]


def lanes_of(shape):
    return lax.broadcasted_iota(I32, shape, len(shape) - 1)


def turn(x, by):
    by %= 128
    return pltpu.roll(x, by, x.ndim - 1) if by else x


def along(x, idx, axis):
    return jnp.take_along_axis(x, idx, axis=axis, mode="promise_in_bounds")


def cross(a, b):
    return [a[1] * b[2] - a[2] * b[1], a[2] * b[0] - a[0] * b[2], a[0] * b[1] - a[1] * b[0]]


def brick_kernel(
    frac, vel, cen_in, counts_in, points_in, active_in, start_in, mass_in, inertia_in,
    fout, curv, mult, motion,
    cen, counts, points, active, rigid, mass, inertia, ED, ER, EC, WT, A, AT, SM, CB, RM, T,
    F, QU, QD, RQL, RQH, PL, PR, RL, RR, RZ, RZF, SQ, HB, HP, HX, HY, HC, HS, HN, HM,
    in_sem, send, recv, hsend, hrecv,
):
    gx, gy, gz = (lax.axis_index(a) for a in ("gx", "gy", "gz"))

    def place(dx, dy, dz):
        return (lax.rem(gx + dx + 16, 16), lax.rem(gy + dy + 8, 8), gz if dz == 0 else 1 - gz)

    everyone = [(dx, dy, dz) for dz in (0, 1) for dx, dy in ACROSS] + [(0, 0, 1)]
    own = []
    for side in (0, 1):
        own.append(pltpu.make_async_copy(vel, T.at[side, :, 4:20, 8:40, :], in_sem.at[2 * side]))
        own.append(pltpu.make_async_copy(frac, F.at[side, 4:20, 8:40, :], in_sem.at[2 * side + 1]))
    for c in own:
        c.start()
    small = [
        pltpu.make_async_copy(src, dst, in_sem.at[4 + k])
        for k, (src, dst) in enumerate((
            (points_in, points), (active_in, active), (start_in, rigid), (mass_in, mass),
            (inertia_in, inertia), (cen_in, cen), (counts_in, counts),
        ))
    ]
    for c in small:
        c.start()

    barrier = pltpu.get_barrier_semaphore()
    for off in everyone:
        pl.semaphore_signal(barrier, inc=1, device_id=place(*off), device_id_type=MESH)

    low = 12 * (1 - gz)
    copies = {}
    count = [0]

    def start(key, src, dst, off):
        k = count[0]
        count[0] += 1
        c = pltpu.make_async_remote_copy(
            src_ref=src, dst_ref=dst, send_sem=send.at[k], recv_sem=recv.at[k], device_id=place(*off),
            device_id_type=MESH,
        )
        c.start()
        copies[key] = c

    for c in own:
        c.wait()

    def pack_rows(g, _):
        for dd in range(4):
            for c in range(3):
                at = 10 * dd + 3 * c
                QU[g, at : at + 3, :] = T[1, c, 4 + 4 * g + dd, 37:40, :]
                QD[g, at : at + 3, :] = T[1, c, 4 + 4 * g + dd, 8:11, :]
            at = 10 * dd + 9
            QU[g, at : at + 1, :] = F[1, 4 + 4 * g + dd, 39:40, :]
            QD[g, at : at + 1, :] = F[1, 4 + 4 * g + dd, 8:9, :]
        return 0

    lax.fori_loop(0, 4, pack_rows, 0)
    pl.semaphore_wait(barrier, len(everyone))
    for dx, src, dst in ((1, QU, RQL), (-1, QD, RQH)):
        start((dx, 0, 0), src, dst.at[1:5], (dx, 0, 0))
        start((dx, 0, 1), src.at[3 * (1 - gz)], dst.at[5 * gz], (dx, 0, 1))

    start("z", vel.at[:, pl.ds(low, 4)], RZ, (0, 0, 1))
    start("zf", frac.at[pl.ds(low, 4)], RZF, (0, 0, 1))

    lane = lanes_of((8, 128))
    spot = lane // 8
    first = (lane % 8) < 4

    def pack_lanes(t, _):
        rows = pl.ds(pl.multiple_of(8 + 8 * t, 8), 8)
        both = []
        for g in range(4):
            acc = None
            for i in range(16):
                c, d = i // 4, 4 + 4 * g + i % 4
                v = turn(T[1, c, d, rows, :] if c < 3 else F[1, d, rows, :], 8 * i + 4)
                acc = v if i == 0 else jnp.where(spot == i, v, acc)
            both.append(acc)
        for h in range(2):
            a, b = both[2 * h], both[2 * h + 1]
            PL[h, t] = jnp.where(first, a, turn(b, 4))
            PR[h, t] = jnp.where(first, turn(a, -4), b)
        return 0

    lax.fori_loop(0, 4, pack_lanes, 0)
    for dy, src, dst in ((1, PL, RL), (-1, PR, RR)):
        for dx in (0, 1, -1):
            ts, td = {0: (slice(0, 4), slice(1, 5)), 1: (3, 0), -1: (0, 5)}[dx]
            start((dx, dy, 0), src.at[:, ts], dst.at[1:3, td], (dx, dy, 0))
            start((dx, dy, 1), src.at[1 - gz, ts], dst.at[3 * gz, td], (dx, dy, 1))

    RQL[5 * gz] = jnp.zeros((40, 128), F32)
    RQH[5 * gz] = jnp.zeros((40, 128), F32)
    RL[3 * gz] = jnp.zeros((6, 8, 128), F32)
    RR[3 * gz] = jnp.zeros((6, 8, 128), F32)
    blank = jnp.zeros((4, 32, 128), F32)
    for side in (0, 1):
        for c in range(3):
            T[side, c, pl.ds(20 * gz, 4), 8:40, :] = blank
        F[side, pl.ds(20 * gz, 4), 8:40, :] = blank

    for c in small:
        c.wait()
    A[...] = jnp.zeros((128, 128), F32)
    A[0:6, :] = rigid[...]
    A[6:7, :] = mass[...]
    A[7:8, :] = inertia[...]
    AT[...] = A[...].T
    owned = counts[0]
    ones = jnp.ones((256, 128), jnp.bfloat16)

    def total(x):
        return jnp.dot(x.astype(jnp.bfloat16), ones[:128], preferred_element_type=F32)

    def prepare(k, _):
        base = pl.multiple_of(32 * k, 32)
        rows = pl.ds(base, 32)
        code = points[rows, :]
        ed = (code * 1338) >> 16
        rest = code - ed * 49
        er = (rest * 9363) >> 16
        ec = rest - er * 7
        ED[rows, :] = ed
        ER[rows, :] = er
        EC[rows, :] = ec
        alive = ((lax.broadcasted_iota(I32, (32, 128), 0) + base) < owned).astype(F32)
        w = active[rows, :].astype(F32) * alive
        WT[rows, :] = w
        e = [(x - 3).astype(F32) for x in (ed, er, ec)]
        we = [w * x for x in e]
        m0 = total(w)
        m1 = [total(x) for x in we]
        m2 = {(i, j): total(we[i] * e[j]) for i in range(3) for j in range(i, 3)}
        J = [m2[(1, 1)] + m2[(2, 2)], m2[(0, 0)] + m2[(2, 2)], m2[(0, 0)] + m2[(1, 1)]]
        columns = AT[rows, :]
        column = [jnp.broadcast_to(columns[:, c : c + 1], (32, 128)) for c in range(8)]
        for c, x in enumerate(column + [m0] + m1 + J + [m2[(0, 1)], m2[(0, 2)], m2[(1, 2)]]):
            CB[c, rows, :] = x
        force, torque = pull(column[0:3], column[3:6], m0, m1, J, m2[(0, 1)], m2[(0, 2)], m2[(1, 2)])
        for c, x in enumerate(force + torque):
            CB[18 + c, rows, :] = x
        return 0

    def pull(linear, angular, m0, m1, J, xy, xz, yz):
        turned = cross(angular, m1)
        force = [m0 * linear[c] + turned[c] for c in range(3)]
        lever = cross(m1, linear)
        torque = [
            lever[0] + (J[0] * angular[0] - xy * angular[1] - xz * angular[2]),
            lever[1] + (J[1] * angular[1] - xy * angular[0] - yz * angular[2]),
            lever[2] + (J[2] * angular[2] - xz * angular[0] - yz * angular[1]),
        ]
        return force, torque

    lax.fori_loop(0, 4, prepare, 0)
    copies["z"].wait()
    copies["zf"].wait()
    for side in (0, 1):
        for c in range(3):
            T[side, c, pl.ds(20 * (1 - gz), 4), 8:40, :] = RZ[c]
        F[side, pl.ds(20 * (1 - gz), 4), 8:40, :] = RZF[...]

    in_low, in_high = (gx > 0).astype(F32), (gx < 15).astype(F32)
    in_left, in_right = (gy > 0).astype(F32), (gy < 7).astype(F32)
    for dx, src, to, here in ((1, RQL, 5, in_low), (-1, RQH, 40, in_high)):
        copies[(dx, 0, 0)].wait()
        copies[(dx, 0, 1)].wait()

        def unpack_rows(g, _):
            for dd in range(4):
                for c in range(3):
                    at = 10 * dd + 3 * c
                    v = src[g, at : at + 3, :] * here
                    T[0, c, 4 * g + dd, to : to + 3, :] = v
                    T[1, c, 4 * g + dd, to : to + 3, :] = v
                at = 10 * dd + 9
                v = src[g, at : at + 1, :] * here
                one = 7 if to == 5 else 40
                F[0, 4 * g + dd, one : one + 1, :] = v
                F[1, 4 * g + dd, one : one + 1, :] = v
            return 0

        lax.fori_loop(0, 6, unpack_rows, 0)

    for dy in (1, -1):
        for dx in (0, 1, -1):
            copies[(dx, dy, 0)].wait()
            copies[(dx, dy, 1)].wait()

    outer_left, outer_right = lane >= 96, lane < 32

    def unpack_lanes(t, _):
        rows = pl.ds(pl.multiple_of(8 * t, 8), 8)
        here = jnp.where(t == 0, in_low, jnp.where(t == 5, in_high, 1.0))
        left, right = in_left * here, in_right * here
        for s in range(4):
            a, b = RL[s, t] * left, RR[s, t] * right
            for part in (0, 1):
                g = 2 * s - 1 + part
                if g < 0 or g > 5:
                    continue
                v = jnp.where(first, a, turn(b, 4)) if part == 0 else jnp.where(first, turn(a, -4), b)
                for i in range(16):
                    c, d = i // 4, 4 * g + i % 4
                    if d in (0, 23):
                        continue
                    w = turn(v, 124 - 8 * i)
                    if c < 3:
                        T[0, c, d, rows, :] = jnp.where(outer_left, w, T[0, c, d, rows, :])
                        T[1, c, d, rows, :] = jnp.where(outer_right, w, T[1, c, d, rows, :])
                    else:
                        F[0, d, rows, :] = jnp.where(outer_left, w, F[0, d, rows, :])
                        F[1, d, rows, :] = jnp.where(outer_right, w, F[1, d, rows, :])
        return 0

    lax.fori_loop(0, 6, unpack_lanes, 0)

    wide = lanes_of((32, 128))
    right_half = wide >= 64
    head, tail = wide == 0, wide == 127

    def flux_of(speed, below, above):
        return jnp.maximum(speed, 0.0) * below + jnp.minimum(speed, 0.0) * above

    def swept(q, flux_low, flux_high, speed_low, speed_high):
        return q - (flux_high - flux_low) + q * (speed_high - speed_low)

    def two(read):
        a, b = read(0), read(1)
        return jnp.where(right_half, b, a), jnp.where(right_half, a, b)

    def sweep_xy(k, _):
        d = 3 + k
        q3 = [two(lambda s, o=o: F[s, d, 7 + o : 39 + o, :]) for o in range(3)]
        u3 = [two(lambda s, o=o: T[s, 1, d, 7 + o : 39 + o, :]) for o in range(3)]
        done = []
        for which in (0, 1):
            q, u = [x[which] for x in q3], [x[which] for x in u3]
            lo, hi = 0.5 * (u[0] + u[1]), 0.5 * (u[1] + u[2])
            done.append(swept(q[1], flux_of(lo, q[0], q[1]), flux_of(hi, q[1], q[2]), lo, hi))
        q, qh = done
        u, uh = two(lambda s: T[s, 2, d, 8:40, :])
        ql, ul = turn(jnp.where(tail, qh, q), 1), turn(jnp.where(tail, uh, u), 1)
        qr, ur = turn(jnp.where(head, qh, q), -1), turn(jnp.where(head, uh, u), -1)
        lo, hi = 0.5 * (ul + u), 0.5 * (u + ur)
        SQ[k] = swept(q, flux_of(lo, ql, q), flux_of(hi, q, qr), lo, hi)
        return 0

    lax.fori_loop(0, 18, sweep_xy, 0)

    HB[...] = jnp.zeros((32, 128), F32)

    def sweep_z(k, _):
        q = [SQ[k + o] for o in range(3)]
        u = [two(lambda s, o=o: T[s, 0, 3 + k + o, 8:40, :])[0] for o in range(3)]
        lo, hi = 0.5 * (u[0] + u[1]), 0.5 * (u[1] + u[2])
        new = swept(q[1], flux_of(lo, q[0], q[1]), flux_of(hi, q[1], q[2]), lo, hi)
        fout[k] = new
        HB[...] += new
        return 0

    lax.fori_loop(0, 16, sweep_z, 0)

    heights = []
    for j, (dx, dy, dz) in enumerate(everyone):
        rows = {0: slice(0, 32), 1: slice(24, 32), -1: slice(0, 8)}[dx]
        if dx == 0 and dy == 0:
            dst = HP
        elif dy == 0:
            dst = HX.at[dz, (dx < 0) * 1]
        elif dx == 0:
            dst = HY.at[dz, (dy < 0) * 1]
        else:
            dst = HC.at[dz, (dx < 0) * 2 + (dy < 0) * 1]
        c = pltpu.make_async_remote_copy(
            src_ref=HB.at[rows], dst_ref=dst, send_sem=hsend.at[j], recv_sem=hrecv.at[j],
            device_id=place(dx, dy, dz), device_id_type=MESH,
        )
        c.start()
        heights.append(c)

    row8 = lax.broadcasted_iota(I32, (8, 128), 0)

    def sample(g, _):
        base = pl.multiple_of(g * GROUP, GROUP)
        tiles = [[None] * (GROUP // 8) for _ in range(3)]
        for s in range(GROUP):
            q = base + s
            d0 = jnp.clip(cen[0, q] - 2, 1, 16)
            r0 = jnp.clip(cen[1, q] + 2, 5, 36)
            jc = cen[2, q] - 3
            side = (jc >= 64).astype(I32)
            e_d = jnp.broadcast_to(ED[pl.ds(q, 1), :], (8, 128))
            e_r = jnp.broadcast_to(ER[pl.ds(q, 1), :], (8, 128))
            idx = (jnp.broadcast_to(EC[pl.ds(q, 1), :], (8, 128)) + (jc - 3)) & 127
            picks = [e_d == k for k in range(1, 7)]
            for c in range(3):
                acc = None
                for k in range(7):
                    v = along(T[side, c, d0 + k, pl.ds(r0, 8), :], idx, 1)
                    acc = v if k == 0 else jnp.where(picks[k - 1], v, acc)
                res = along(acc, e_r, 0)
                old = tiles[c][s // 8]
                tiles[c][s // 8] = res if s % 8 == 0 else jnp.where(row8 == s % 8, res, old)
        for c in range(3):
            SM[c, pl.ds(base, GROUP), :] = jnp.concatenate(tiles[c], axis=0)
        return 0

    lax.fori_loop(0, 128 // GROUP, sample, 0)

    def total_of(x):
        high = x.astype(jnp.bfloat16)
        rest = (x - high.astype(F32)).astype(jnp.bfloat16)
        return jnp.dot(jnp.concatenate([high, rest], axis=1), ones, preferred_element_type=F32)

    def iterate(k, _):
        rows = pl.ds(pl.multiple_of(32 * k, 32), 32)
        s = [SM[c, rows, :] for c in range(3)]
        w = WT[rows, :]
        e = [(x[rows, :] - 3).astype(F32) for x in (ED, ER, EC)]
        ws = [w * x for x in s]
        S = [total_of(x) for x in ws]
        Q = [total_of(x) for x in cross(e, ws)]
        n = [CB[c, rows, :] for c in range(24)]
        linear, angular, force, torque = n[0:3], n[3:6], n[18:21], n[21:24]
        linear1 = [linear[c] + n[6] * (S[c] - force[c]) for c in range(3)]
        angular1 = [angular[c] + n[7] * (Q[c] - torque[c]) for c in range(3)]
        force1, torque1 = pull(linear1, angular1, n[8], n[9:12], n[12:15], n[15], n[16], n[17])
        last = [linear[c] + n[6] * (1.5 * S[c] - 0.5 * force[c] - force1[c]) for c in range(3)]
        last += [angular[c] + n[7] * (1.5 * Q[c] - 0.5 * torque[c] - torque1[c]) for c in range(3)]
        both = [0.5 * linear[c] + linear1[c] for c in range(3)]
        spin = cross([0.5 * angular[c] + angular1[c] for c in range(3)], e)
        for c in range(3):
            mult[c, rows, :] = 1.5 * ws[c] - w * (both[c] + spin[c])
        lanes = lanes_of((32, 128))
        out = jnp.zeros((32, 128), F32)
        for c in range(6):
            out = jnp.where(lanes == c, last[c], out)
        alive = ((lax.broadcasted_iota(I32, (32, 128), 0) + 32 * k) < owned).astype(F32)
        RM[rows, :] = out * alive
        return 0

    lax.fori_loop(0, 4, iterate, 0)
    motion[...] = RM[...].T[0:6, :]

    for c in heights:
        c.wait()

    HS[0, 8:40] = HB[...] + HP[...]
    HS[0, 0:8] = (HX[0, 0] + HX[1, 0]) * in_low
    HS[0, 40:48] = (HX[0, 1] + HX[1, 1]) * in_high
    HS[1, 8:40] = jnp.where(
        right_half, (HY[0, 0] + HY[1, 0]) * in_left, (HY[0, 1] + HY[1, 1]) * in_right
    )
    for x, at, here in ((0, 0, in_low), (1, 40, in_high)):
        HS[1, at : at + 8] = jnp.where(
            lane >= 64,
            (HC[0, 2 * x] + HC[1, 2 * x]) * (in_left * here),
            (HC[0, 2 * x + 1] + HC[1, 2 * x + 1]) * (in_right * here),
        )
    all_lanes = lanes_of((48, 128))
    h, hh = HS[0], HS[1]
    HN[...] = turn(jnp.where(all_lanes == 0, hh, h), -1)
    HM[...] = turn(jnp.where(all_lanes == 127, hh, h), 1)
    middle, east, west = HS[0, 8:40], HS[0, 9:41], HS[0, 7:39]
    north, south = HN[8:40], HM[8:40]
    slope_x, slope_y = 0.5 * (east - west), 0.5 * (north - south)
    bend_xx = east - 2.0 * middle + west
    bend_yy = north - 2.0 * middle + south
    bend_xy = 0.25 * (HN[9:41] - HM[9:41] - HN[7:39] + HM[7:39])
    metric = 1.0 + slope_x * slope_x + slope_y * slope_y
    top = (
        bend_xx * (1.0 + slope_y * slope_y) + bend_yy * (1.0 + slope_x * slope_x)
        - 2.0 * slope_x * slope_y * bend_xy
    )
    curv[...] = top / (metric * jnp.sqrt(metric))


def pass_kernel(*refs):
    n = (len(refs) - 1) // 2
    moves = [pltpu.make_async_copy(refs[k], refs[n + k], refs[-1].at[k]) for k in range(n)]
    for c in moves:
        c.start()
    for c in moves:
        c.wait()


def body(fraction, velocity, centres, points, active_points, counts, rigid_start, mass, inertia):
    vmem, anywhere = pl.BlockSpec(memory_space=pltpu.VMEM), pl.BlockSpec(memory_space=pl.ANY)
    hbm = pl.BlockSpec(memory_space=pltpu.HBM)

    def f32(*shape):
        return jax.ShapeDtypeStruct(shape, F32)

    def room(*shape, dtype=F32):
        return pltpu.VMEM(shape, dtype)

    outs = (f32(16, 32, 128), f32(32, 128), f32(3, 128, 128), f32(6, 128))
    results = pl.pallas_call(
        brick_kernel,
        out_shape=outs,
        in_specs=[hbm] * 9,
        out_specs=(vmem,) * 4,
        scratch_shapes=[
            pltpu.SMEM((3, 128), I32), pltpu.SMEM((1,), I32),
            room(128, 128, dtype=I32), room(128, 128, dtype=I32), room(6, 128), room(1, 128), room(1, 128),
            room(128, 128, dtype=I32), room(128, 128, dtype=I32), room(128, 128, dtype=I32),
            room(128, 128), room(128, 128), room(128, 128), room(3, 128, 128), room(24, 128, 128), room(128, 128),
            room(2, 3, 24, 48, 128), room(2, 24, 48, 128),
            room(4, 40, 128), room(4, 40, 128), room(6, 40, 128), room(6, 40, 128),
            room(2, 4, 8, 128), room(2, 4, 8, 128), room(4, 6, 8, 128), room(4, 6, 8, 128),
            room(3, 4, 32, 128), room(4, 32, 128), room(18, 32, 128),
            room(32, 128), room(32, 128), room(2, 2, 8, 128), room(2, 2, 32, 128), room(2, 4, 8, 128),
            room(2, 48, 128), room(48, 128), room(48, 128),
            pltpu.SemaphoreType.DMA((11,)),
            pltpu.SemaphoreType.DMA((18,)), pltpu.SemaphoreType.DMA((18,)),
            pltpu.SemaphoreType.DMA((17,)), pltpu.SemaphoreType.DMA((17,)),
        ],
        compiler_params=pltpu.CompilerParams(
            collective_id=0, has_side_effects=True, vmem_limit_bytes=60 << 20
        ),
        name="brick",
    )(
        fraction, velocity, centres, counts, points, active_points, rigid_start,
        mass.reshape(1, 128), inertia.reshape(1, 128),
    )
    return pl.pallas_call(
        pass_kernel,
        out_shape=outs,
        in_specs=[vmem] * 4,
        out_specs=(hbm,) * 4,
        scratch_shapes=[pltpu.SemaphoreType.DMA((4,))],
        name="pass_on",
    )(*results)


def solution(mesh):
    bricks = ("gx", "gy", "gz")
    placed = (
        P("gz", "gx", "gy"), P(None, "gz", "gx", "gy"), P(None, bricks), P(bricks, None), P(bricks, None),
        P(bricks), P(None, bricks), P(bricks), P(bricks),
    )
    return jax.shard_map(
        body, mesh=mesh, in_specs=placed,
        out_specs=(P("gz", "gx", "gy"), P("gx", "gy"), P(None, bricks, None), P(None, bricks)),
        check_vma=False,
    )
```

```python
import jax
import jax.numpy as jnp
from jax import lax
from jax.experimental import pallas as pl
from jax.experimental.pallas import tpu as pltpu
from jax.sharding import PartitionSpec as P

MESH = pl.DeviceIdType.MESH
GROUP = 16
F32 = jnp.float32
I32 = jnp.int32

ACROSS = [(dx, dy) for dx in (-1, 0, 1) for dy in (-1, 0, 1) if dx or dy]


def lanes_of(shape):
    return lax.broadcasted_iota(I32, shape, len(shape) - 1)


def turn(x, by):
    by %= 128
    return pltpu.roll(x, by, x.ndim - 1) if by else x


def along(x, idx, axis):
    return jnp.take_along_axis(x, idx, axis=axis, mode="promise_in_bounds")


def cross(a, b):
    return [a[1] * b[2] - a[2] * b[1], a[2] * b[0] - a[0] * b[2], a[0] * b[1] - a[1] * b[0]]


def brick_kernel(
    frac, vel, cen_in, counts, points_in, active_in, start_in, mass_in, inertia_in,
    fout, curv, mult, motion,
    cen, points, active, rigid, mass, inertia, ED, ER, EC, WT, A, AT, SM, CB, RM, T,
    F, QU, QD, RQL, RQH, PL, PR, RL, RR, RZ, RZF, SQ, HB, HP, HX, HY, HC, HS, HN, HM,
    in_sem, send, recv, hsend, hrecv,
):
    gx, gy, gz = (lax.axis_index(a) for a in ("gx", "gy", "gz"))

    def place(dx, dy, dz):
        return (lax.rem(gx + dx + 16, 16), lax.rem(gy + dy + 8, 8), gz if dz == 0 else 1 - gz)

    everyone = [(dx, dy, dz) for dz in (0, 1) for dx, dy in ACROSS] + [(0, 0, 1)]
    own = []
    for side in (0, 1):
        own.append(pltpu.make_async_copy(vel, T.at[side, :, 4:20, 8:40, :], in_sem.at[2 * side]))
        own.append(pltpu.make_async_copy(frac, F.at[side, 4:20, 8:40, :], in_sem.at[2 * side + 1]))
    for c in own:
        c.start()
    small = [
        pltpu.make_async_copy(src, dst, in_sem.at[4 + k])
        for k, (src, dst) in enumerate((
            (points_in, points), (active_in, active), (start_in, rigid), (mass_in, mass),
            (inertia_in, inertia), (cen_in, cen),
        ))
    ]
    for c in small:
        c.start()

    barrier = pltpu.get_barrier_semaphore()
    for off in everyone:
        pl.semaphore_signal(barrier, inc=1, device_id=place(*off), device_id_type=MESH)

    low = 12 * (1 - gz)
    copies = {}
    count = [0]

    def start(key, src, dst, off):
        k = count[0]
        count[0] += 1
        c = pltpu.make_async_remote_copy(
            src_ref=src, dst_ref=dst, send_sem=send.at[k], recv_sem=recv.at[k], device_id=place(*off),
            device_id_type=MESH,
        )
        c.start()
        copies[key] = c

    for c in own:
        c.wait()

    def pack_rows(g, _):
        for dd in range(4):
            for c in range(3):
                at = 10 * dd + 3 * c
                QU[g, at : at + 3, :] = T[1, c, 4 + 4 * g + dd, 37:40, :]
                QD[g, at : at + 3, :] = T[1, c, 4 + 4 * g + dd, 8:11, :]
            at = 10 * dd + 9
            QU[g, at : at + 1, :] = F[1, 4 + 4 * g + dd, 39:40, :]
            QD[g, at : at + 1, :] = F[1, 4 + 4 * g + dd, 8:9, :]
        return 0

    lax.fori_loop(0, 4, pack_rows, 0)
    pl.semaphore_wait(barrier, len(everyone))
    for dx, src, dst in ((1, QU, RQL), (-1, QD, RQH)):
        start((dx, 0, 0), src, dst.at[1:5], (dx, 0, 0))
        start((dx, 0, 1), src.at[3 * (1 - gz)], dst.at[5 * gz], (dx, 0, 1))

    start("z", vel.at[:, pl.ds(low, 4)], RZ, (0, 0, 1))
    start("zf", frac.at[pl.ds(low, 4)], RZF, (0, 0, 1))

    lane = lanes_of((8, 128))
    spot = lane // 8
    first = (lane % 8) < 4

    def pack_lanes(t, _):
        rows = pl.ds(pl.multiple_of(8 + 8 * t, 8), 8)
        both = []
        for g in range(4):
            acc = None
            for i in range(16):
                c, d = i // 4, 4 + 4 * g + i % 4
                v = turn(T[1, c, d, rows, :] if c < 3 else F[1, d, rows, :], 8 * i + 4)
                acc = v if i == 0 else jnp.where(spot == i, v, acc)
            both.append(acc)
        for h in range(2):
            a, b = both[2 * h], both[2 * h + 1]
            PL[h, t] = jnp.where(first, a, turn(b, 4))
            PR[h, t] = jnp.where(first, turn(a, -4), b)
        return 0

    lax.fori_loop(0, 4, pack_lanes, 0)
    for dy, src, dst in ((1, PL, RL), (-1, PR, RR)):
        for dx in (0, 1, -1):
            ts, td = {0: (slice(0, 4), slice(1, 5)), 1: (3, 0), -1: (0, 5)}[dx]
            start((dx, dy, 0), src.at[:, ts], dst.at[1:3, td], (dx, dy, 0))
            start((dx, dy, 1), src.at[1 - gz, ts], dst.at[3 * gz, td], (dx, dy, 1))

    RQL[5 * gz] = jnp.zeros((40, 128), F32)
    RQH[5 * gz] = jnp.zeros((40, 128), F32)
    RL[3 * gz] = jnp.zeros((6, 8, 128), F32)
    RR[3 * gz] = jnp.zeros((6, 8, 128), F32)
    blank = jnp.zeros((4, 32, 128), F32)
    for side in (0, 1):
        for c in range(3):
            T[side, c, pl.ds(20 * gz, 4), 8:40, :] = blank
        F[side, pl.ds(20 * gz, 4), 8:40, :] = blank

    for c in small:
        c.wait()
    A[...] = jnp.zeros((128, 128), F32)
    A[0:6, :] = rigid[...]
    A[6:7, :] = mass[...]
    A[7:8, :] = inertia[...]
    AT[...] = A[...].T
    owned = counts[0]
    ones = jnp.ones((256, 128), jnp.bfloat16)

    def total(x):
        return jnp.dot(x.astype(jnp.bfloat16), ones[:128], preferred_element_type=F32)

    def prepare(k, _):
        base = pl.multiple_of(32 * k, 32)
        rows = pl.ds(base, 32)
        code = points[rows, :]
        ed = (code * 1338) >> 16
        rest = code - ed * 49
        er = (rest * 9363) >> 16
        ec = rest - er * 7
        ED[rows, :] = ed
        ER[rows, :] = er
        EC[rows, :] = ec
        alive = ((lax.broadcasted_iota(I32, (32, 128), 0) + base) < owned).astype(F32)
        w = active[rows, :].astype(F32) * alive
        WT[rows, :] = w
        e = [(x - 3).astype(F32) for x in (ed, er, ec)]
        we = [w * x for x in e]
        m0 = total(w)
        m1 = [total(x) for x in we]
        m2 = {(i, j): total(we[i] * e[j]) for i in range(3) for j in range(i, 3)}
        J = [m2[(1, 1)] + m2[(2, 2)], m2[(0, 0)] + m2[(2, 2)], m2[(0, 0)] + m2[(1, 1)]]
        columns = AT[rows, :]
        column = [jnp.broadcast_to(columns[:, c : c + 1], (32, 128)) for c in range(8)]
        for c, x in enumerate(column + [m0] + m1 + J + [m2[(0, 1)], m2[(0, 2)], m2[(1, 2)]]):
            CB[c, rows, :] = x
        force, torque = pull(column[0:3], column[3:6], m0, m1, J, m2[(0, 1)], m2[(0, 2)], m2[(1, 2)])
        for c, x in enumerate(force + torque):
            CB[18 + c, rows, :] = x
        return 0

    def pull(linear, angular, m0, m1, J, xy, xz, yz):
        turned = cross(angular, m1)
        force = [m0 * linear[c] + turned[c] for c in range(3)]
        lever = cross(m1, linear)
        torque = [
            lever[0] + (J[0] * angular[0] - xy * angular[1] - xz * angular[2]),
            lever[1] + (J[1] * angular[1] - xy * angular[0] - yz * angular[2]),
            lever[2] + (J[2] * angular[2] - xz * angular[0] - yz * angular[1]),
        ]
        return force, torque

    lax.fori_loop(0, 4, prepare, 0)
    copies["z"].wait()
    copies["zf"].wait()
    for side in (0, 1):
        for c in range(3):
            T[side, c, pl.ds(20 * (1 - gz), 4), 8:40, :] = RZ[c]
        F[side, pl.ds(20 * (1 - gz), 4), 8:40, :] = RZF[...]

    in_low, in_high = (gx > 0).astype(F32), (gx < 15).astype(F32)
    in_left, in_right = (gy > 0).astype(F32), (gy < 7).astype(F32)
    for dx, src, to, here in ((1, RQL, 5, in_low), (-1, RQH, 40, in_high)):
        copies[(dx, 0, 0)].wait()
        copies[(dx, 0, 1)].wait()

        def unpack_rows(g, _):
            for dd in range(4):
                for c in range(3):
                    at = 10 * dd + 3 * c
                    v = src[g, at : at + 3, :] * here
                    T[0, c, 4 * g + dd, to : to + 3, :] = v
                    T[1, c, 4 * g + dd, to : to + 3, :] = v
                at = 10 * dd + 9
                v = src[g, at : at + 1, :] * here
                one = 7 if to == 5 else 40
                F[0, 4 * g + dd, one : one + 1, :] = v
                F[1, 4 * g + dd, one : one + 1, :] = v
            return 0

        lax.fori_loop(0, 6, unpack_rows, 0)

    for dy in (1, -1):
        for dx in (0, 1, -1):
            copies[(dx, dy, 0)].wait()
            copies[(dx, dy, 1)].wait()

    outer_left, outer_right = lane >= 96, lane < 32

    def unpack_lanes(t, _):
        rows = pl.ds(pl.multiple_of(8 * t, 8), 8)
        here = jnp.where(t == 0, in_low, jnp.where(t == 5, in_high, 1.0))
        left, right = in_left * here, in_right * here
        for s in range(4):
            a, b = RL[s, t] * left, RR[s, t] * right
            for part in (0, 1):
                g = 2 * s - 1 + part
                if g < 0 or g > 5:
                    continue
                v = jnp.where(first, a, turn(b, 4)) if part == 0 else jnp.where(first, turn(a, -4), b)
                for i in range(16):
                    c, d = i // 4, 4 * g + i % 4
                    if d in (0, 23):
                        continue
                    w = turn(v, 124 - 8 * i)
                    if c < 3:
                        T[0, c, d, rows, :] = jnp.where(outer_left, w, T[0, c, d, rows, :])
                        T[1, c, d, rows, :] = jnp.where(outer_right, w, T[1, c, d, rows, :])
                    else:
                        F[0, d, rows, :] = jnp.where(outer_left, w, F[0, d, rows, :])
                        F[1, d, rows, :] = jnp.where(outer_right, w, F[1, d, rows, :])
        return 0

    lax.fori_loop(0, 6, unpack_lanes, 0)

    wide = lanes_of((32, 128))
    right_half = wide >= 64
    head, tail = wide == 0, wide == 127

    def flux_of(speed, below, above):
        return jnp.maximum(speed, 0.0) * below + jnp.minimum(speed, 0.0) * above

    def swept(q, flux_low, flux_high, speed_low, speed_high):
        return q - (flux_high - flux_low) + q * (speed_high - speed_low)

    def two(read):
        a, b = read(0), read(1)
        return jnp.where(right_half, b, a), jnp.where(right_half, a, b)

    def sweep_xy(k, _):
        d = 3 + k
        q3 = [two(lambda s, o=o: F[s, d, 7 + o : 39 + o, :]) for o in range(3)]
        u3 = [two(lambda s, o=o: T[s, 1, d, 7 + o : 39 + o, :]) for o in range(3)]
        done = []
        for which in (0, 1):
            q, u = [x[which] for x in q3], [x[which] for x in u3]
            lo, hi = 0.5 * (u[0] + u[1]), 0.5 * (u[1] + u[2])
            done.append(swept(q[1], flux_of(lo, q[0], q[1]), flux_of(hi, q[1], q[2]), lo, hi))
        q, qh = done
        u, uh = two(lambda s: T[s, 2, d, 8:40, :])
        ql, ul = turn(jnp.where(tail, qh, q), 1), turn(jnp.where(tail, uh, u), 1)
        qr, ur = turn(jnp.where(head, qh, q), -1), turn(jnp.where(head, uh, u), -1)
        lo, hi = 0.5 * (ul + u), 0.5 * (u + ur)
        SQ[k] = swept(q, flux_of(lo, ql, q), flux_of(hi, q, qr), lo, hi)
        return 0

    lax.fori_loop(0, 18, sweep_xy, 0)

    HB[...] = jnp.zeros((32, 128), F32)

    def sweep_z(k, _):
        q = [SQ[k + o] for o in range(3)]
        u = [two(lambda s, o=o: T[s, 0, 3 + k + o, 8:40, :])[0] for o in range(3)]
        lo, hi = 0.5 * (u[0] + u[1]), 0.5 * (u[1] + u[2])
        new = swept(q[1], flux_of(lo, q[0], q[1]), flux_of(hi, q[1], q[2]), lo, hi)
        fout[k] = new
        HB[...] += new
        return 0

    lax.fori_loop(0, 16, sweep_z, 0)

    heights = []
    for j, (dx, dy, dz) in enumerate(everyone):
        rows = {0: slice(0, 32), 1: slice(24, 32), -1: slice(0, 8)}[dx]
        if dx == 0 and dy == 0:
            dst = HP
        elif dy == 0:
            dst = HX.at[dz, (dx < 0) * 1]
        elif dx == 0:
            dst = HY.at[dz, (dy < 0) * 1]
        else:
            dst = HC.at[dz, (dx < 0) * 2 + (dy < 0) * 1]
        c = pltpu.make_async_remote_copy(
            src_ref=HB.at[rows], dst_ref=dst, send_sem=hsend.at[j], recv_sem=hrecv.at[j],
            device_id=place(dx, dy, dz), device_id_type=MESH,
        )
        c.start()
        heights.append(c)

    row8 = lax.broadcasted_iota(I32, (8, 128), 0)

    def sample(g, _):
        base = pl.multiple_of(g * GROUP, GROUP)
        tiles = [[None] * (GROUP // 8) for _ in range(3)]
        for s in range(GROUP):
            q = base + s
            d0 = jnp.clip(cen[0, q] - 2, 1, 16)
            r0 = jnp.clip(cen[1, q] + 2, 5, 36)
            jc = cen[2, q] - 3
            side = (jc >= 64).astype(I32)
            e_d = jnp.broadcast_to(ED[pl.ds(q, 1), :], (8, 128))
            e_r = jnp.broadcast_to(ER[pl.ds(q, 1), :], (8, 128))
            idx = (jnp.broadcast_to(EC[pl.ds(q, 1), :], (8, 128)) + (jc - 3)) & 127
            picks = [e_d == k for k in range(1, 7)]
            for c in range(3):
                acc = None
                for k in range(7):
                    v = along(T[side, c, d0 + k, pl.ds(r0, 8), :], idx, 1)
                    acc = v if k == 0 else jnp.where(picks[k - 1], v, acc)
                res = along(acc, e_r, 0)
                old = tiles[c][s // 8]
                tiles[c][s // 8] = res if s % 8 == 0 else jnp.where(row8 == s % 8, res, old)
        for c in range(3):
            SM[c, pl.ds(base, GROUP), :] = jnp.concatenate(tiles[c], axis=0)
        return 0

    lax.fori_loop(0, 128 // GROUP, sample, 0)

    def total_of(x):
        high = x.astype(jnp.bfloat16)
        rest = (x - high.astype(F32)).astype(jnp.bfloat16)
        return jnp.dot(jnp.concatenate([high, rest], axis=1), ones, preferred_element_type=F32)

    def iterate(k, _):
        rows = pl.ds(pl.multiple_of(32 * k, 32), 32)
        s = [SM[c, rows, :] for c in range(3)]
        w = WT[rows, :]
        e = [(x[rows, :] - 3).astype(F32) for x in (ED, ER, EC)]
        ws = [w * x for x in s]
        S = [total_of(x) for x in ws]
        Q = [total_of(x) for x in cross(e, ws)]
        n = [CB[c, rows, :] for c in range(24)]
        linear, angular, force, torque = n[0:3], n[3:6], n[18:21], n[21:24]
        linear1 = [linear[c] + n[6] * (S[c] - force[c]) for c in range(3)]
        angular1 = [angular[c] + n[7] * (Q[c] - torque[c]) for c in range(3)]
        force1, torque1 = pull(linear1, angular1, n[8], n[9:12], n[12:15], n[15], n[16], n[17])
        last = [linear[c] + n[6] * (1.5 * S[c] - 0.5 * force[c] - force1[c]) for c in range(3)]
        last += [angular[c] + n[7] * (1.5 * Q[c] - 0.5 * torque[c] - torque1[c]) for c in range(3)]
        both = [0.5 * linear[c] + linear1[c] for c in range(3)]
        spin = cross([0.5 * angular[c] + angular1[c] for c in range(3)], e)
        for c in range(3):
            mult[c, rows, :] = 1.5 * ws[c] - w * (both[c] + spin[c])
        lanes = lanes_of((32, 128))
        out = jnp.zeros((32, 128), F32)
        for c in range(6):
            out = jnp.where(lanes == c, last[c], out)
        alive = ((lax.broadcasted_iota(I32, (32, 128), 0) + 32 * k) < owned).astype(F32)
        RM[rows, :] = out * alive
        return 0

    lax.fori_loop(0, 4, iterate, 0)
    motion[...] = RM[...].T[0:6, :]

    for c in heights:
        c.wait()

    HS[0, 8:40] = HB[...] + HP[...]
    HS[0, 0:8] = (HX[0, 0] + HX[1, 0]) * in_low
    HS[0, 40:48] = (HX[0, 1] + HX[1, 1]) * in_high
    HS[1, 8:40] = jnp.where(
        right_half, (HY[0, 0] + HY[1, 0]) * in_left, (HY[0, 1] + HY[1, 1]) * in_right
    )
    for x, at, here in ((0, 0, in_low), (1, 40, in_high)):
        HS[1, at : at + 8] = jnp.where(
            lane >= 64,
            (HC[0, 2 * x] + HC[1, 2 * x]) * (in_left * here),
            (HC[0, 2 * x + 1] + HC[1, 2 * x + 1]) * (in_right * here),
        )
    all_lanes = lanes_of((48, 128))
    h, hh = HS[0], HS[1]
    HN[...] = turn(jnp.where(all_lanes == 0, hh, h), -1)
    HM[...] = turn(jnp.where(all_lanes == 127, hh, h), 1)
    middle, east, west = HS[0, 8:40], HS[0, 9:41], HS[0, 7:39]
    north, south = HN[8:40], HM[8:40]
    slope_x, slope_y = 0.5 * (east - west), 0.5 * (north - south)
    bend_xx = east - 2.0 * middle + west
    bend_yy = north - 2.0 * middle + south
    bend_xy = 0.25 * (HN[9:41] - HM[9:41] - HN[7:39] + HM[7:39])
    metric = 1.0 + slope_x * slope_x + slope_y * slope_y
    top = (
        bend_xx * (1.0 + slope_y * slope_y) + bend_yy * (1.0 + slope_x * slope_x)
        - 2.0 * slope_x * slope_y * bend_xy
    )
    curv[...] = top / (metric * jnp.sqrt(metric))


def pinned(x):
    return pltpu.with_memory_space_constraint(x, pltpu.HBM)


def pass_kernel(*refs):
    n = (len(refs) - 1) // 2
    moves = [pltpu.make_async_copy(refs[k], refs[n + k], refs[-1].at[k]) for k in range(n)]
    for c in moves:
        c.start()
    for c in moves:
        c.wait()


def body(fraction, velocity, centres, points, active_points, counts, rigid_start, mass, inertia):
    vmem, anywhere = pl.BlockSpec(memory_space=pltpu.VMEM), pl.BlockSpec(memory_space=pl.ANY)
    hbm = pl.BlockSpec(memory_space=pltpu.HBM)

    def f32(*shape):
        return jax.ShapeDtypeStruct(shape, F32)

    def room(*shape, dtype=F32):
        return pltpu.VMEM(shape, dtype)

    outs = (f32(16, 32, 128), f32(32, 128), f32(3, 128, 128), f32(6, 128))
    results = pl.pallas_call(
        brick_kernel,
        out_shape=outs,
        in_specs=[hbm] * 3 + [pl.BlockSpec(memory_space=pltpu.SMEM)] + [hbm] * 5,
        out_specs=(vmem,) * 4,
        scratch_shapes=[
            pltpu.SMEM((3, 128), I32),
            room(128, 128, dtype=I32), room(128, 128, dtype=I32), room(6, 128), room(1, 128), room(1, 128),
            room(128, 128, dtype=I32), room(128, 128, dtype=I32), room(128, 128, dtype=I32),
            room(128, 128), room(128, 128), room(128, 128), room(3, 128, 128), room(24, 128, 128), room(128, 128),
            room(2, 3, 24, 48, 128), room(2, 24, 48, 128),
            room(4, 40, 128), room(4, 40, 128), room(6, 40, 128), room(6, 40, 128),
            room(2, 4, 8, 128), room(2, 4, 8, 128), room(4, 6, 8, 128), room(4, 6, 8, 128),
            room(3, 4, 32, 128), room(4, 32, 128), room(18, 32, 128),
            room(32, 128), room(32, 128), room(2, 2, 8, 128), room(2, 2, 32, 128), room(2, 4, 8, 128),
            room(2, 48, 128), room(48, 128), room(48, 128),
            pltpu.SemaphoreType.DMA((10,)),
            pltpu.SemaphoreType.DMA((18,)), pltpu.SemaphoreType.DMA((18,)),
            pltpu.SemaphoreType.DMA((17,)), pltpu.SemaphoreType.DMA((17,)),
        ],
        compiler_params=pltpu.CompilerParams(
            collective_id=0, has_side_effects=True, vmem_limit_bytes=40 << 20
        ),
        name="brick",
    )(
        *(pinned(x) for x in (fraction, velocity, centres)), counts,
        *(pinned(x) for x in (points, active_points, rigid_start, mass.reshape(1, 128), inertia.reshape(1, 128))),
    )
    return pl.pallas_call(
        pass_kernel,
        out_shape=outs,
        in_specs=[anywhere] * 4,
        out_specs=(hbm,) * 4,
        scratch_shapes=[pltpu.SemaphoreType.DMA((4,))],
        compiler_params=pltpu.CompilerParams(vmem_limit_bytes=4 << 20),
        name="pass_on",
    )(*results)


def solution(mesh):
    bricks = ("gx", "gy", "gz")
    placed = (
        P("gz", "gx", "gy"), P(None, "gz", "gx", "gy"), P(None, bricks), P(bricks, None), P(bricks, None),
        P(bricks), P(None, bricks), P(bricks), P(bricks),
    )
    return jax.shard_map(
        body, mesh=mesh, in_specs=placed,
        out_specs=(P("gz", "gx", "gy"), P("gx", "gy"), P(None, bricks, None), P(None, bricks)),
        check_vma=False,
    )
```

```python
import jax
import jax.numpy as jnp
from jax import lax
from jax.experimental import pallas as pl
from jax.experimental.pallas import tpu as pltpu
from jax.sharding import PartitionSpec as P

MESH = pl.DeviceIdType.MESH
GROUP = 16
F32 = jnp.float32
I32 = jnp.int32

ACROSS = [(dx, dy) for dx in (-1, 0, 1) for dy in (-1, 0, 1) if dx or dy]


def lanes_of(shape):
    return lax.broadcasted_iota(I32, shape, len(shape) - 1)


def loop(steps, step, per=1):
    def some(g, _):
        for j in range(per):
            step(g * per + j, 0)
        return 0

    if steps == per:
        for k in range(steps):
            step(k, 0)
    else:
        lax.fori_loop(0, steps // per, some, 0)


def rows8(first):
    return pl.ds(first if isinstance(first, int) else pl.multiple_of(first, 8), 8)


def turn(x, by):
    by %= 128
    return pltpu.roll(x, by, x.ndim - 1) if by else x


def along(x, idx, axis):
    return jnp.take_along_axis(x, idx, axis=axis, mode="promise_in_bounds")


def cross(a, b):
    return [a[1] * b[2] - a[2] * b[1], a[2] * b[0] - a[0] * b[2], a[0] * b[1] - a[1] * b[0]]


def brick_kernel(
    frac, vel, cen_in, counts, points_in, active_in, start_in, mass_in, inertia_in,
    fout, curv, mult, motion,
    cen, points, active, rigid, mass, inertia, ED, ER, EC, WT, A, AT, SM, CB, RM, T,
    F, QU, QD, RQL, RQH, RV, PL, PR, RL, RR, PH, PV, SH, SQ, HB, HP, HY, HS, HN, HM,
    in_sem, send, recv, hsend, hrecv,
):
    gx, gy, gz = (lax.axis_index(a) for a in ("gx", "gy", "gz"))

    def place(dx, dy, dz):
        return (lax.rem(gx + dx + 16, 16), lax.rem(gy + dy + 8, 8), gz if dz == 0 else 1 - gz)

    everyone = [(dx, dy, dz) for dz in (0, 1) for dx, dy in ACROSS] + [(0, 0, 1)]
    own = [
        pltpu.make_async_copy(vel, T.at[0, :, 4:20, 8:40, :], in_sem.at[0]),
        pltpu.make_async_copy(frac, F.at[4:20, 8:40, :], in_sem.at[1]),
    ]
    for c in own:
        c.start()
    small = [
        pltpu.make_async_copy(src, dst, in_sem.at[2 + k])
        for k, (src, dst) in enumerate((
            (points_in, points), (active_in, active), (start_in, rigid), (mass_in, mass),
            (inertia_in, inertia), (cen_in, cen),
        ))
    ]
    for c in small:
        c.start()

    barrier = pltpu.get_barrier_semaphore()
    for off in everyone:
        pl.semaphore_signal(barrier, inc=1, device_id=place(*off), device_id_type=MESH)

    low = 12 * (1 - gz)
    copies = {}
    count = [0]

    def start(key, src, dst, off):
        k = count[0]
        count[0] += 1
        c = pltpu.make_async_remote_copy(
            src_ref=src, dst_ref=dst, send_sem=send.at[k], recv_sem=recv.at[k], device_id=place(*off),
            device_id_type=MESH,
        )
        c.start()
        copies[key] = c

    for c in own:
        c.wait()

    def layers(c, d):
        return T.at[0, c, d] if c < 3 else F.at[d]

    def pack_rows(g, _):
        for dd in range(4):
            for c in range(4):
                at = 12 * dd + 3 * c
                QU[g, at : at + 3, :] = layers(c, 4 + 4 * g + dd)[37:40, :]
                QD[g, at : at + 3, :] = layers(c, 4 + 4 * g + dd)[8:11, :]
        return 0

    loop(4, pack_rows, 1)
    pl.semaphore_wait(barrier, len(everyone))
    for dx, src, dst in ((1, QU, RQL), (-1, QD, RQH)):
        start((dx, 0, 0), src, dst.at[1:5], (dx, 0, 0))
        start((dx, 0, 1), src.at[3 * (1 - gz)], dst.at[5 * gz], (dx, 0, 1))

    start("z", vel.at[:, pl.ds(low, 4)], T.at[0, :, pl.ds(20 * gz, 4), 8:40, :], (0, 0, 1))
    start("zf", frac.at[pl.ds(low, 4)], F.at[pl.ds(20 * gz, 4), 8:40, :], (0, 0, 1))

    lane = lanes_of((8, 128))
    spot = lane // 8
    first = (lane % 8) < 4

    def pack_lanes(t, _):
        rows = rows8(8 + 8 * t)
        both = []
        for c in range(4):
            acc = None
            for d in range(16):
                v = turn(layers(c, 4 + d)[rows, :], 8 * d + 4)
                acc = v if d == 0 else jnp.where(spot == d, v, acc)
            both.append(acc)
        for h in range(2):
            a, b = both[2 * h], both[2 * h + 1]
            PL[h, t] = jnp.where(first, a, turn(b, 4))
            PR[h, t] = jnp.where(first, turn(a, -4), b)
        return 0

    loop(4, pack_lanes, 4)
    for dx in (0, 1, -1):
        ts, td = {0: (slice(0, 4), slice(1, 5)), 1: (3, 0), -1: (0, 5)}[dx]
        for dz in (0, 1):
            for dy, src, dst in ((1, PL, RL), (-1, PR, RR)):
                start((dx, dy, dz), src.at[:, ts], dst.at[2 * gz if dz else 1, :, td], (dx, dy, dz))

    RQL[5 * gz] = jnp.zeros((48, 128), F32)
    RQH[5 * gz] = jnp.zeros((48, 128), F32)
    RL[2 * gz] = jnp.zeros((2, 6, 8, 128), F32)
    RR[2 * gz] = jnp.zeros((2, 6, 8, 128), F32)
    blank = jnp.zeros((4, 32, 128), F32)
    for c in range(3):
        T[0, c, pl.ds(20 * gz, 4), 8:40, :] = blank
        T[1, c, pl.ds(20 * gz, 4), 8:40, :] = blank
    F[pl.ds(20 * gz, 4), 8:40, :] = blank

    def aside(x):
        return jnp.where(lanes_of(x.shape) < 64, turn(x, 60), turn(x, 68))

    def fill_aside(k, _):
        for c in range(3):
            T[1, c, 4 + k, 8:40, :] = aside(T[0, c, 4 + k, 8:40, :])
        return 0

    loop(16, fill_aside, 4)

    for c in small:
        c.wait()
    A[...] = jnp.zeros((128, 128), F32)
    A[0:6, :] = rigid[...]
    A[6:7, :] = mass[...]
    A[7:8, :] = inertia[...]
    AT[...] = A[...].T
    owned = counts[0]
    ones = jnp.ones((256, 128), jnp.bfloat16)

    def total(x):
        return jnp.dot(x.astype(jnp.bfloat16), ones[:128], preferred_element_type=F32)

    def prepare(k, _):
        base = pl.multiple_of(32 * k, 32)
        rows = pl.ds(base, 32)
        code = points[rows, :]
        ed = (code * 1338) >> 16
        rest = code - ed * 49
        er = (rest * 9363) >> 16
        ec = rest - er * 7
        ED[rows, :] = ed
        ER[rows, :] = er
        EC[rows, :] = ec
        alive = ((lax.broadcasted_iota(I32, (32, 128), 0) + base) < owned).astype(F32)
        w = active[rows, :].astype(F32) * alive
        WT[rows, :] = w
        e = [(x - 3).astype(F32) for x in (ed, er, ec)]
        we = [w * x for x in e]
        m0 = total(w)
        m1 = [total(x) for x in we]
        m2 = {(i, j): total(we[i] * e[j]) for i in range(3) for j in range(i, 3)}
        J = [m2[(1, 1)] + m2[(2, 2)], m2[(0, 0)] + m2[(2, 2)], m2[(0, 0)] + m2[(1, 1)]]
        columns = AT[rows, :]
        column = [jnp.broadcast_to(columns[:, c : c + 1], (32, 128)) for c in range(8)]
        for c, x in enumerate(column + [m0] + m1 + J + [m2[(0, 1)], m2[(0, 2)], m2[(1, 2)]]):
            CB[c, rows, :] = x
        force, torque = pull(column[0:3], column[3:6], m0, m1, J, m2[(0, 1)], m2[(0, 2)], m2[(1, 2)])
        for c, x in enumerate(force + torque):
            CB[18 + c, rows, :] = x
        return 0

    def pull(linear, angular, m0, m1, J, xy, xz, yz):
        turned = cross(angular, m1)
        force = [m0 * linear[c] + turned[c] for c in range(3)]
        lever = cross(m1, linear)
        torque = [
            lever[0] + (J[0] * angular[0] - xy * angular[1] - xz * angular[2]),
            lever[1] + (J[1] * angular[1] - xy * angular[0] - yz * angular[2]),
            lever[2] + (J[2] * angular[2] - xz * angular[0] - yz * angular[1]),
        ]
        return force, torque

    loop(4, prepare, 2)
    copies["z"].wait()
    copies["zf"].wait()

    def fill_aside_partner(k, _):
        for c in range(3):
            T[1, c, 20 * (1 - gz) + k, 8:40, :] = aside(T[0, c, 20 * (1 - gz) + k, 8:40, :])
        return 0

    loop(4, fill_aside_partner, 4)

    in_low, in_high = (gx > 0).astype(F32), (gx < 15).astype(F32)
    in_left, in_right = (gy > 0).astype(F32), (gy < 7).astype(F32)
    ranks = ((1, RQL, 5, in_low), (-1, RQH, 40, in_high))
    for dx, src, to, here in ranks:
        copies[(dx, 0, 0)].wait()
        copies[(dx, 0, 1)].wait()

        def unpack_rows(g, _):
            for dd in range(4):
                for c in range(4):
                    at = 12 * dd + 3 * c
                    layers(c, 4 * g + dd)[to : to + 3, :] = src[g, at : at + 3, :] * here
            return 0

        loop(6, unpack_rows, 2)

    for dy in (1, -1):
        for dx in (0, 1, -1):
            copies[(dx, dy, 0)].wait()
            copies[(dx, dy, 1)].wait()

    def merge(t, _):
        rows = rows8(8 * t)
        here = jnp.where(t == 0, in_low, jnp.where(t == 5, in_high, 1.0))
        left, right = in_left * here, in_right * here
        for lev in range(3):
            for c in range(4):
                a, b = RL[lev, c // 2, t] * left, RR[lev, c // 2, t] * right
                if c > 0:
                    PH[c - 1, lev, rows, :] = (
                        jnp.where(first, turn(a, -4), b) if c % 2 else jnp.where(first, a, turn(b, 4))
                    )
                if c < 3:
                    PV[c, lev, rows, :] = (
                        jnp.where(first, turn(b, -4), a) if c % 2 else jnp.where(first, b, turn(a, 4))
                    )
        return 0

    loop(6, merge, 3)

    wide = lanes_of((40, 128))
    head, tail = wide == 0, wide == 127

    def flux_of(speed, below, above):
        return jnp.maximum(speed, 0.0) * below + jnp.minimum(speed, 0.0) * above

    def swept(q, flux_low, flux_high, speed_low, speed_high):
        return q - (flux_high - flux_low) + q * (speed_high - speed_low)

    def sweep_of(q, u):
        lo, hi = 0.5 * (u[0] + u[1]), 0.5 * (u[1] + u[2])
        return swept(q[1], flux_of(lo, q[0], q[1]), flux_of(hi, q[1], q[2]), lo, hi)

    for lev in range(3):
        SH[lev] = sweep_of(
            [PH[2, lev, 6 + o : 46 + o, :] for o in range(3)], [PH[0, lev, 6 + o : 46 + o, :] for o in range(3)]
        )

    def sweep_xy(k, _):
        d = 3 + k
        q = sweep_of(
            [F[d, 6 + o : 46 + o, :] for o in range(3)], [T[0, 1, d, 6 + o : 46 + o, :] for o in range(3)]
        )
        u = T[0, 2, d, 7:47, :]
        lev = jnp.where(k == 0, 0, jnp.where(k == 17, 2, 1))
        by = 124 - 8 * ((k + 15) % 16)
        qh, uh = pltpu.roll(SH[lev], by, 1), pltpu.roll(PH[1, lev, 7:47, :], by, 1)
        ql, ul = turn(jnp.where(tail, qh, q), 1), turn(jnp.where(tail, uh, u), 1)
        qr, ur = turn(jnp.where(head, qh, q), -1), turn(jnp.where(head, uh, u), -1)
        SQ[k] = sweep_of([ql, q, qr], [ul, u, ur])
        return 0

    loop(18, sweep_xy, 6)

    def sweep_z(k, carry):
        total_height, q, u, speed, flux = carry
        above, u_above = SQ[k + 2], T[0, 0, 5 + k, 7:47, :]
        speed_above = 0.5 * (u + u_above)
        flux_above = flux_of(speed_above, q, above)
        new = swept(q, flux, flux_above, speed, speed_above)
        fout[k, 7:47, :] = new
        return total_height + new, above, u_above, speed_above, flux_above

    u0, u1 = T[0, 0, 3, 7:47, :], T[0, 0, 4, 7:47, :]
    speed0 = 0.5 * (u0 + u1)
    HB[...] = lax.fori_loop(
        0, 16, sweep_z, (jnp.zeros((40, 128), F32), SQ[1], u1, speed0, flux_of(speed0, SQ[0], SQ[1]))
    )[0]

    heights = []
    for j, (dy, dz) in enumerate([(1, 1), (-1, 1), (1, 0), (-1, 0), (0, 1)]):
        c = pltpu.make_async_remote_copy(
            src_ref=HB, dst_ref=HY.at[dz, (dy < 0) * 1] if dy else HP, send_sem=hsend.at[j], recv_sem=hrecv.at[j],
            device_id=place(0, dy, dz), device_id_type=MESH,
        )
        c.start()
        heights.append(c)

    for dx, src, to, here in ranks:
        def shift_rows(g, _):
            RV[g] = aside(src[g] * here)
            return 0

        def place_rows(g, _):
            for dd in range(4):
                for c in range(3):
                    at = 12 * dd + 3 * c
                    T[1, c, 4 * g + dd, to : to + 3, :] = RV[g, at : at + 3, :]
            return 0

        loop(6, shift_rows, 3)
        loop(6, place_rows, 2)
    joint = (lane >= 60) & (lane < 68)

    def unpack_lanes(t, _):
        rows = rows8(8 * t)
        for c in range(3):
            for lev, near in ((0, range(13, 16)), (1, range(16)), (2, range(3))):
                v = PV[c, lev, rows, :]
                for d in near:
                    at = 4 + 16 * (lev - 1) + d
                    pltpu.store(T.at[1, c, at, rows, :], turn(v, 60 - 8 * d), mask=joint)
        return 0

    loop(6, unpack_lanes, 1)

    row8 = lax.broadcasted_iota(I32, (8, 128), 0)

    def sample(g, _):
        base = pl.multiple_of(g * GROUP, GROUP)
        tiles = [[None] * (GROUP // 8) for _ in range(3)]
        for s in range(GROUP):
            q = base + s
            d0 = jnp.clip(cen[0, q] - 2, 1, 16)
            r0 = jnp.clip(cen[1, q] + 2, 5, 36)
            jc = cen[2, q] - 3
            at_left, at_right = (jc < 3).astype(I32), (jc > 124).astype(I32)
            side = at_left + at_right
            first_lane = jc - 3 + 68 * (at_left - at_right)
            e_d = jnp.broadcast_to(ED[pl.ds(q, 1), :], (8, 128))
            e_r = jnp.broadcast_to(ER[pl.ds(q, 1), :], (8, 128))
            idx = (jnp.broadcast_to(EC[pl.ds(q, 1), :], (8, 128)) + first_lane) & 127
            picks = [e_d == k for k in range(1, 7)]
            for c in range(3):
                acc = None
                for k in range(7):
                    v = along(T[side, c, d0 + k, pl.ds(r0, 8), :], idx, 1)
                    acc = v if k == 0 else jnp.where(picks[k - 1], v, acc)
                res = along(acc, e_r, 0)
                old = tiles[c][s // 8]
                tiles[c][s // 8] = res if s % 8 == 0 else jnp.where(row8 == s % 8, res, old)
        for c in range(3):
            SM[c, pl.ds(base, GROUP), :] = jnp.concatenate(tiles[c], axis=0)
        return 0

    loop(128 // GROUP, sample, 1)

    def total_of(x):
        high = x.astype(jnp.bfloat16)
        rest = (x - high.astype(F32)).astype(jnp.bfloat16)
        return jnp.dot(jnp.concatenate([high, rest], axis=1), ones, preferred_element_type=F32)

    def iterate(k, _):
        rows = pl.ds(pl.multiple_of(32 * k, 32), 32)
        s = [SM[c, rows, :] for c in range(3)]
        w = WT[rows, :]
        e = [(x[rows, :] - 3).astype(F32) for x in (ED, ER, EC)]
        ws = [w * x for x in s]
        S = [total_of(x) for x in ws]
        Q = [total_of(x) for x in cross(e, ws)]
        n = [CB[c, rows, :] for c in range(24)]
        linear, angular, force, torque = n[0:3], n[3:6], n[18:21], n[21:24]
        linear1 = [linear[c] + n[6] * (S[c] - force[c]) for c in range(3)]
        angular1 = [angular[c] + n[7] * (Q[c] - torque[c]) for c in range(3)]
        force1, torque1 = pull(linear1, angular1, n[8], n[9:12], n[12:15], n[15], n[16], n[17])
        last = [linear[c] + n[6] * (1.5 * S[c] - 0.5 * force[c] - force1[c]) for c in range(3)]
        last += [angular[c] + n[7] * (1.5 * Q[c] - 0.5 * torque[c] - torque1[c]) for c in range(3)]
        both = [0.5 * linear[c] + linear1[c] for c in range(3)]
        spin = cross([0.5 * angular[c] + angular1[c] for c in range(3)], e)
        for c in range(3):
            mult[c, rows, :] = 1.5 * ws[c] - w * (both[c] + spin[c])
        lanes = lanes_of((32, 128))
        out = jnp.zeros((32, 128), F32)
        for c in range(6):
            out = jnp.where(lanes == c, last[c], out)
        alive = ((lax.broadcasted_iota(I32, (32, 128), 0) + 32 * k) < owned).astype(F32)
        RM[rows, :] = out * alive
        return 0

    loop(4, iterate, 2)
    motion[...] = RM[...].T[0:6, :]

    for c in heights:
        c.wait()

    row = lax.broadcasted_iota(I32, (40, 128), 0)
    inside = jnp.where(row == 0, in_low, jnp.where(row == 33, in_high, 1.0))
    h = (HB[...] + HP[...]) * inside
    hh = jnp.where(wide >= 64, (HY[0, 0] + HY[1, 0]) * in_left, (HY[0, 1] + HY[1, 1]) * in_right) * inside
    HS[...] = h
    HN[...] = turn(jnp.where(head, hh, h), -1)
    HM[...] = turn(jnp.where(tail, hh, h), 1)
    middle, east, west = HS[1:33], HS[2:34], HS[0:32]
    north, south = HN[1:33], HM[1:33]
    slope_x, slope_y = 0.5 * (east - west), 0.5 * (north - south)
    bend_xx = east - 2.0 * middle + west
    bend_yy = north - 2.0 * middle + south
    bend_xy = 0.25 * (HN[2:34] - HM[2:34] - HN[0:32] + HM[0:32])
    metric = 1.0 + slope_x * slope_x + slope_y * slope_y
    top = (
        bend_xx * (1.0 + slope_y * slope_y) + bend_yy * (1.0 + slope_x * slope_x)
        - 2.0 * slope_x * slope_y * bend_xy
    )
    curv[...] = top / (metric * jnp.sqrt(metric))


def pinned(x):
    return pltpu.with_memory_space_constraint(x, pltpu.HBM)


def pass_kernel(*refs):
    n = (len(refs) - 1) // 2
    sources = [refs[0].at[:, 8:40, :]] + list(refs[1:n])
    moves = [pltpu.make_async_copy(sources[k], refs[n + k], refs[-1].at[k]) for k in range(n)]
    for c in moves:
        c.start()
    for c in moves:
        c.wait()


def body(fraction, velocity, centres, points, active_points, counts, rigid_start, mass, inertia):
    vmem, anywhere = pl.BlockSpec(memory_space=pltpu.VMEM), pl.BlockSpec(memory_space=pl.ANY)
    hbm = pl.BlockSpec(memory_space=pltpu.HBM)

    def f32(*shape):
        return jax.ShapeDtypeStruct(shape, F32)

    def room(*shape, dtype=F32):
        return pltpu.VMEM(shape, dtype)

    outs = (f32(16, 32, 128), f32(32, 128), f32(3, 128, 128), f32(6, 128))
    results = pl.pallas_call(
        brick_kernel,
        out_shape=(f32(16, 48, 128),) + outs[1:],
        in_specs=[hbm] * 3 + [pl.BlockSpec(memory_space=pltpu.SMEM)] + [hbm] * 5,
        out_specs=(vmem,) * 4,
        scratch_shapes=[
            pltpu.SMEM((3, 128), I32),
            room(128, 128, dtype=I32), room(128, 128, dtype=I32), room(6, 128), room(1, 128), room(1, 128),
            room(128, 128, dtype=I32), room(128, 128, dtype=I32), room(128, 128, dtype=I32),
            room(128, 128), room(128, 128), room(128, 128), room(3, 128, 128), room(24, 128, 128), room(128, 128),
            room(2, 3, 24, 48, 128), room(24, 48, 128),
            room(4, 48, 128), room(4, 48, 128), room(6, 48, 128), room(6, 48, 128), room(6, 48, 128),
            room(2, 4, 8, 128), room(2, 4, 8, 128), room(3, 2, 6, 8, 128), room(3, 2, 6, 8, 128),
            room(3, 3, 48, 128), room(3, 3, 48, 128), room(3, 40, 128), room(18, 40, 128),
            room(40, 128), room(40, 128), room(2, 2, 40, 128), room(40, 128), room(40, 128), room(40, 128),
            pltpu.SemaphoreType.DMA((8,)),
            pltpu.SemaphoreType.DMA((18,)), pltpu.SemaphoreType.DMA((18,)),
            pltpu.SemaphoreType.DMA((5,)), pltpu.SemaphoreType.DMA((5,)),
        ],
        compiler_params=pltpu.CompilerParams(
            collective_id=0, has_side_effects=True, vmem_limit_bytes=40 << 20
        ),
        name="brick",
    )(
        *(pinned(x) for x in (fraction, velocity, centres)), counts,
        *(pinned(x) for x in (points, active_points, rigid_start, mass.reshape(1, 128), inertia.reshape(1, 128))),
    )
    return pl.pallas_call(
        pass_kernel,
        out_shape=outs,
        in_specs=[anywhere] * 4,
        out_specs=(hbm,) * 4,
        scratch_shapes=[pltpu.SemaphoreType.DMA((4,))],
        compiler_params=pltpu.CompilerParams(vmem_limit_bytes=4 << 20),
        name="pass_on",
    )(*results)


def solution(mesh):
    bricks = ("gx", "gy", "gz")
    placed = (
        P("gz", "gx", "gy"), P(None, "gz", "gx", "gy"), P(None, bricks), P(bricks, None), P(bricks, None),
        P(bricks), P(None, bricks), P(bricks), P(bricks),
    )
    return jax.shard_map(
        body, mesh=mesh, in_specs=placed,
        out_specs=(P("gz", "gx", "gy"), P("gx", "gy"), P(None, bricks, None), P(None, bricks)),
        check_vma=False,
    )
```

```python
import jax
import jax.numpy as jnp
from jax import lax
from jax.experimental import pallas as pl
from jax.experimental.pallas import tpu as pltpu
from jax.sharding import PartitionSpec as P

MESH = pl.DeviceIdType.MESH
GROUP = 64
F32 = jnp.float32
I32 = jnp.int32

ACROSS = [(dx, dy) for dx in (-1, 0, 1) for dy in (-1, 0, 1) if dx or dy]


def lanes_of(shape):
    return lax.broadcasted_iota(I32, shape, len(shape) - 1)


def loop(steps, step, per=1):
    def some(g, _):
        for j in range(per):
            step(g * per + j, 0)
        return 0

    if steps == per:
        for k in range(steps):
            step(k, 0)
    else:
        lax.fori_loop(0, steps // per, some, 0)


def rows8(first):
    return pl.ds(first if isinstance(first, int) else pl.multiple_of(first, 8), 8)


def turn(x, by):
    by %= 128
    return pltpu.roll(x, by, x.ndim - 1) if by else x


def along(x, idx, axis):
    return jnp.take_along_axis(x, idx, axis=axis, mode="promise_in_bounds")


def cross(a, b):
    return [a[1] * b[2] - a[2] * b[1], a[2] * b[0] - a[0] * b[2], a[0] * b[1] - a[1] * b[0]]


def brick_kernel(
    frac, vel, cen_in, counts, points_in, active_in, start_in, mass_in, inertia_in,
    fout, curv, mult, motion,
    cen, points, active, rigid, mass, inertia, ED, ER, EC, WT, A, AT, SM, CB, RM, T,
    F, QU, QD, RQL, RQH, RV, PL, PR, RL, RR, PH, PV, SH, SQ, HB, HP, HY, HS, HN, HM,
    in_sem, send, recv, hsend, hrecv,
):
    gx, gy, gz = (lax.axis_index(a) for a in ("gx", "gy", "gz"))

    def place(dx, dy, dz):
        return (lax.rem(gx + dx + 16, 16), lax.rem(gy + dy + 8, 8), gz if dz == 0 else 1 - gz)

    everyone = [(dx, dy, dz) for dz in (0, 1) for dx, dy in ACROSS] + [(0, 0, 1)]
    own = [
        pltpu.make_async_copy(vel, T.at[0, :, 4:20, 8:40, :], in_sem.at[0]),
        pltpu.make_async_copy(frac, F.at[4:20, 8:40, :], in_sem.at[1]),
    ]
    for c in own:
        c.start()
    barrier = pltpu.get_barrier_semaphore()
    for off in everyone:
        pl.semaphore_signal(barrier, inc=1, device_id=place(*off), device_id_type=MESH)

    small = [
        pltpu.make_async_copy(src, dst, in_sem.at[2 + k])
        for k, (src, dst) in enumerate((
            (points_in, points), (active_in, active), (start_in, rigid), (mass_in, mass),
            (inertia_in, inertia), (cen_in, cen),
        ))
    ]
    for c in small:
        c.start()

    low = 12 * (1 - gz)
    copies = {}
    count = [0]

    def start(key, src, dst, off):
        k = count[0]
        count[0] += 1
        c = pltpu.make_async_remote_copy(
            src_ref=src, dst_ref=dst, send_sem=send.at[k], recv_sem=recv.at[k], device_id=place(*off),
            device_id_type=MESH,
        )
        c.start()
        copies[key] = c

    for c in own:
        c.wait()

    def layers(c, d):
        return T.at[0, c, d] if c < 3 else F.at[d]

    def pack_rows(g, _):
        for dd in range(4):
            for c in range(4):
                at = 12 * dd + 3 * c
                QU[g, at : at + 3, :] = layers(c, 4 + 4 * g + dd)[37:40, :]
                QD[g, at : at + 3, :] = layers(c, 4 + 4 * g + dd)[8:11, :]
        return 0

    loop(4, pack_rows, 1)
    pl.semaphore_wait(barrier, len(everyone))
    for dx, src, dst in ((1, QU, RQL), (-1, QD, RQH)):
        start((dx, 0, 0), src, dst.at[1:5], (dx, 0, 0))
        start((dx, 0, 1), src.at[3 * (1 - gz)], dst.at[5 * gz], (dx, 0, 1))

    start("z", vel.at[:, pl.ds(low, 4)], T.at[0, :, pl.ds(20 * gz, 4), 8:40, :], (0, 0, 1))
    start("zf", frac.at[pl.ds(low, 4)], F.at[pl.ds(20 * gz, 4), 8:40, :], (0, 0, 1))

    lane = lanes_of((8, 128))
    spot = lane // 8
    first = (lane % 8) < 4

    def pack_lanes(t, _):
        rows = rows8(8 + 8 * t)
        both = []
        for c in range(4):
            acc = None
            for d in range(16):
                v = turn(layers(c, 4 + d)[rows, :], 8 * d + 4)
                acc = v if d == 0 else jnp.where(spot == d, v, acc)
            both.append(acc)
        for h in range(2):
            a, b = both[2 * h], both[2 * h + 1]
            PL[h, t] = jnp.where(first, a, turn(b, 4))
            PR[h, t] = jnp.where(first, turn(a, -4), b)
        return 0

    loop(4, pack_lanes, 4)
    for dx in (0, 1, -1):
        ts, td = {0: (slice(0, 4), slice(1, 5)), 1: (3, 0), -1: (0, 5)}[dx]
        for dz in (0, 1):
            for dy, src, dst in ((1, PL, RL), (-1, PR, RR)):
                start((dx, dy, dz), src.at[:, ts], dst.at[2 * gz if dz else 1, :, td], (dx, dy, dz))

    RQL[5 * gz] = jnp.zeros((48, 128), F32)
    RQH[5 * gz] = jnp.zeros((48, 128), F32)
    RL[2 * gz] = jnp.zeros((2, 6, 8, 128), F32)
    RR[2 * gz] = jnp.zeros((2, 6, 8, 128), F32)
    blank = jnp.zeros((4, 32, 128), F32)
    for c in range(3):
        T[0, c, pl.ds(20 * gz, 4), 8:40, :] = blank
        T[1, c, pl.ds(20 * gz, 4), 8:40, :] = blank
    F[pl.ds(20 * gz, 4), 8:40, :] = blank

    def aside(x):
        return jnp.where(lanes_of(x.shape) < 64, turn(x, 60), turn(x, 68))

    def fill_aside(k, _):
        for c in range(3):
            T[1, c, 4 + k, 8:40, :] = aside(T[0, c, 4 + k, 8:40, :])
        return 0

    loop(16, fill_aside, 4)

    for c in small:
        c.wait()
    A[...] = jnp.zeros((128, 128), F32)
    A[0:6, :] = rigid[...]
    A[6:7, :] = mass[...]
    A[7:8, :] = inertia[...]
    AT[...] = A[...].T
    owned = counts[0]
    ones = jnp.ones((256, 128), jnp.bfloat16)

    def total(x):
        return jnp.dot(x.astype(jnp.bfloat16), ones[:128], preferred_element_type=F32)

    def prepare(k, _):
        base = pl.multiple_of(32 * k, 32)
        rows = pl.ds(base, 32)
        code = points[rows, :]
        ed = (code * 1338) >> 16
        rest = code - ed * 49
        er = (rest * 9363) >> 16
        ec = rest - er * 7
        ED[rows, :] = ed
        ER[rows, :] = er
        EC[rows, :] = ec
        alive = ((lax.broadcasted_iota(I32, (32, 128), 0) + base) < owned).astype(F32)
        w = active[rows, :].astype(F32) * alive
        WT[rows, :] = w
        e = [(x - 3).astype(F32) for x in (ed, er, ec)]
        we = [w * x for x in e]
        m0 = total(w)
        m1 = [total(x) for x in we]
        m2 = {(i, j): total(we[i] * e[j]) for i in range(3) for j in range(i, 3)}
        J = [m2[(1, 1)] + m2[(2, 2)], m2[(0, 0)] + m2[(2, 2)], m2[(0, 0)] + m2[(1, 1)]]
        columns = AT[rows, :]
        column = [jnp.broadcast_to(columns[:, c : c + 1], (32, 128)) for c in range(8)]
        for c, x in enumerate(column + [m0] + m1 + J + [m2[(0, 1)], m2[(0, 2)], m2[(1, 2)]]):
            CB[c, rows, :] = x
        force, torque = pull(column[0:3], column[3:6], m0, m1, J, m2[(0, 1)], m2[(0, 2)], m2[(1, 2)])
        for c, x in enumerate(force + torque):
            CB[18 + c, rows, :] = x
        return 0

    def pull(linear, angular, m0, m1, J, xy, xz, yz):
        turned = cross(angular, m1)
        force = [m0 * linear[c] + turned[c] for c in range(3)]
        lever = cross(m1, linear)
        torque = [
            lever[0] + (J[0] * angular[0] - xy * angular[1] - xz * angular[2]),
            lever[1] + (J[1] * angular[1] - xy * angular[0] - yz * angular[2]),
            lever[2] + (J[2] * angular[2] - xz * angular[0] - yz * angular[1]),
        ]
        return force, torque

    loop(4, prepare, 2)
    copies["z"].wait()
    copies["zf"].wait()

    def fill_aside_partner(k, _):
        for c in range(3):
            T[1, c, 20 * (1 - gz) + k, 8:40, :] = aside(T[0, c, 20 * (1 - gz) + k, 8:40, :])
        return 0

    loop(4, fill_aside_partner, 4)

    in_low, in_high = (gx > 0).astype(F32), (gx < 15).astype(F32)
    in_left, in_right = (gy > 0).astype(F32), (gy < 7).astype(F32)
    ranks = ((1, RQL, 5, in_low), (-1, RQH, 40, in_high))
    for dx, src, to, here in ranks:
        copies[(dx, 0, 0)].wait()
        copies[(dx, 0, 1)].wait()

        def unpack_rows(g, _):
            for dd in range(4):
                for c in range(4):
                    at = 12 * dd + 3 * c
                    layers(c, 4 * g + dd)[to : to + 3, :] = src[g, at : at + 3, :] * here
            return 0

        loop(6, unpack_rows, 2)

    for dx, src, to, here in ranks:
        def shift_rows(g, _):
            RV[g] = aside(src[g] * here)
            return 0

        def place_rows(g, _):
            for dd in range(4):
                for c in range(3):
                    at = 12 * dd + 3 * c
                    T[1, c, 4 * g + dd, to : to + 3, :] = RV[g, at : at + 3, :]
            return 0

        loop(6, shift_rows, 3)
        loop(6, place_rows, 2)

    for dy in (1, -1):
        for dx in (0, 1, -1):
            copies[(dx, dy, 0)].wait()
            copies[(dx, dy, 1)].wait()

    def merge(t, _):
        rows = rows8(8 * t)
        here = jnp.where(t == 0, in_low, jnp.where(t == 5, in_high, 1.0))
        left, right = in_left * here, in_right * here
        for lev in range(3):
            for c in range(4):
                a, b = RL[lev, c // 2, t] * left, RR[lev, c // 2, t] * right
                if c > 0:
                    PH[c - 1, lev, rows, :] = (
                        jnp.where(first, turn(a, -4), b) if c % 2 else jnp.where(first, a, turn(b, 4))
                    )
                if c < 3:
                    PV[c, lev, rows, :] = (
                        jnp.where(first, turn(b, -4), a) if c % 2 else jnp.where(first, b, turn(a, 4))
                    )
        return 0

    loop(6, merge, 3)

    wide = lanes_of((40, 128))
    head, tail = wide == 0, wide == 127

    def flux_of(speed, below, above):
        return jnp.maximum(speed, 0.0) * below + jnp.minimum(speed, 0.0) * above

    def swept(q, flux_low, flux_high, speed_low, speed_high):
        return q - (flux_high - flux_low) + q * (speed_high - speed_low)

    def sweep_of(q, u):
        lo, hi = 0.5 * (u[0] + u[1]), 0.5 * (u[1] + u[2])
        return swept(q[1], flux_of(lo, q[0], q[1]), flux_of(hi, q[1], q[2]), lo, hi)

    for lev in range(3):
        SH[lev] = sweep_of(
            [PH[2, lev, 6 + o : 46 + o, :] for o in range(3)], [PH[0, lev, 6 + o : 46 + o, :] for o in range(3)]
        )

    def sweep_xy(k, _):
        d = 3 + k
        q = sweep_of(
            [F[d, 6 + o : 46 + o, :] for o in range(3)], [T[0, 1, d, 6 + o : 46 + o, :] for o in range(3)]
        )
        u = T[0, 2, d, 7:47, :]
        lev = jnp.where(k == 0, 0, jnp.where(k == 17, 2, 1))
        by = 124 - 8 * ((k + 15) % 16)
        qh, uh = pltpu.roll(SH[lev], by, 1), pltpu.roll(PH[1, lev, 7:47, :], by, 1)
        ql, ul = turn(jnp.where(tail, qh, q), 1), turn(jnp.where(tail, uh, u), 1)
        qr, ur = turn(jnp.where(head, qh, q), -1), turn(jnp.where(head, uh, u), -1)
        SQ[k] = sweep_of([ql, q, qr], [ul, u, ur])
        return 0

    loop(18, sweep_xy, 6)

    def sweep_z(k, carry):
        total_height, q, u, speed, flux = carry
        above, u_above = SQ[k + 2], T[0, 0, 5 + k, 7:47, :]
        speed_above = 0.5 * (u + u_above)
        flux_above = flux_of(speed_above, q, above)
        new = swept(q, flux, flux_above, speed, speed_above)
        fout[k, 7:47, :] = new
        return total_height + new, above, u_above, speed_above, flux_above

    u0, u1 = T[0, 0, 3, 7:47, :], T[0, 0, 4, 7:47, :]
    speed0 = 0.5 * (u0 + u1)
    HB[...] = lax.fori_loop(
        0, 16, sweep_z, (jnp.zeros((40, 128), F32), SQ[1], u1, speed0, flux_of(speed0, SQ[0], SQ[1]))
    )[0]

    heights = []
    for j, (dy, dz) in enumerate([(1, 1), (-1, 1), (1, 0), (-1, 0), (0, 1)]):
        c = pltpu.make_async_remote_copy(
            src_ref=HB, dst_ref=HY.at[dz, (dy < 0) * 1] if dy else HP, send_sem=hsend.at[j], recv_sem=hrecv.at[j],
            device_id=place(0, dy, dz), device_id_type=MESH,
        )
        c.start()
        heights.append(c)

    joint = (lane >= 60) & (lane < 68)

    def unpack_lanes(t, _):
        rows = rows8(8 * t)
        for c in range(3):
            for lev, near in ((0, range(13, 16)), (1, range(16)), (2, range(3))):
                v = PV[c, lev, rows, :]
                for d in near:
                    at = 4 + 16 * (lev - 1) + d
                    pltpu.store(T.at[1, c, at, rows, :], turn(v, 60 - 8 * d), mask=joint)
        return 0

    loop(6, unpack_lanes, 3)

    row8 = lax.broadcasted_iota(I32, (8, 128), 0)

    def sample(g, _):
        base = pl.multiple_of(g * GROUP, GROUP)
        tiles = [[None] * (GROUP // 8) for _ in range(3)]
        for s in range(GROUP):
            q = base + s
            d0 = jnp.clip(cen[0, q] - 2, 1, 16)
            r0 = jnp.clip(cen[1, q] + 2, 5, 36)
            jc = cen[2, q] - 3
            at_left, at_right = (jc < 3).astype(I32), (jc > 124).astype(I32)
            side = at_left + at_right
            first_lane = jc - 3 + 68 * (at_left - at_right)
            e_d = jnp.broadcast_to(ED[pl.ds(q, 1), :], (8, 128))
            e_r = jnp.broadcast_to(ER[pl.ds(q, 1), :], (8, 128))
            idx = (jnp.broadcast_to(EC[pl.ds(q, 1), :], (8, 128)) + first_lane) & 127
            picks = [e_d == k for k in range(1, 7)]
            for c in range(3):
                acc = None
                for k in range(7):
                    v = along(T[side, c, d0 + k, pl.ds(r0, 8), :], idx, 1)
                    acc = v if k == 0 else jnp.where(picks[k - 1], v, acc)
                res = along(acc, e_r, 0)
                old = tiles[c][s // 8]
                tiles[c][s // 8] = res if s % 8 == 0 else jnp.where(row8 == s % 8, res, old)
        for c in range(3):
            SM[c, pl.ds(base, GROUP), :] = jnp.concatenate(tiles[c], axis=0)
        return 0

    loop(128 // GROUP, sample, 1)

    def total_of(x):
        high = x.astype(jnp.bfloat16)
        rest = (x - high.astype(F32)).astype(jnp.bfloat16)
        return jnp.dot(jnp.concatenate([high, rest], axis=1), ones, preferred_element_type=F32)

    def iterate(k, _):
        rows = pl.ds(pl.multiple_of(32 * k, 32), 32)
        s = [SM[c, rows, :] for c in range(3)]
        w = WT[rows, :]
        e = [(x[rows, :] - 3).astype(F32) for x in (ED, ER, EC)]
        ws = [w * x for x in s]
        S = [total_of(x) for x in ws]
        Q = [total_of(x) for x in cross(e, ws)]
        n = [CB[c, rows, :] for c in range(24)]
        linear, angular, force, torque = n[0:3], n[3:6], n[18:21], n[21:24]
        linear1 = [linear[c] + n[6] * (S[c] - force[c]) for c in range(3)]
        angular1 = [angular[c] + n[7] * (Q[c] - torque[c]) for c in range(3)]
        force1, torque1 = pull(linear1, angular1, n[8], n[9:12], n[12:15], n[15], n[16], n[17])
        last = [linear[c] + n[6] * (1.5 * S[c] - 0.5 * force[c] - force1[c]) for c in range(3)]
        last += [angular[c] + n[7] * (1.5 * Q[c] - 0.5 * torque[c] - torque1[c]) for c in range(3)]
        both = [0.5 * linear[c] + linear1[c] for c in range(3)]
        spin = cross([0.5 * angular[c] + angular1[c] for c in range(3)], e)
        for c in range(3):
            mult[c, rows, :] = 1.5 * ws[c] - w * (both[c] + spin[c])
        lanes = lanes_of((32, 128))
        out = jnp.zeros((32, 128), F32)
        for c in range(6):
            out = jnp.where(lanes == c, last[c], out)
        alive = ((lax.broadcasted_iota(I32, (32, 128), 0) + 32 * k) < owned).astype(F32)
        RM[rows, :] = out * alive
        return 0

    loop(4, iterate, 4)
    motion[...] = RM[...].T[0:6, :]

    for c in heights:
        c.wait()

    row = lax.broadcasted_iota(I32, (40, 128), 0)
    inside = jnp.where(row == 0, in_low, jnp.where(row == 33, in_high, 1.0))
    h = (HB[...] + HP[...]) * inside
    hh = jnp.where(wide >= 64, (HY[0, 0] + HY[1, 0]) * in_left, (HY[0, 1] + HY[1, 1]) * in_right) * inside
    HS[...] = h
    HN[...] = turn(jnp.where(head, hh, h), -1)
    HM[...] = turn(jnp.where(tail, hh, h), 1)
    middle, east, west = HS[1:33], HS[2:34], HS[0:32]
    north, south = HN[1:33], HM[1:33]
    slope_x, slope_y = 0.5 * (east - west), 0.5 * (north - south)
    bend_xx = east - 2.0 * middle + west
    bend_yy = north - 2.0 * middle + south
    bend_xy = 0.25 * (HN[2:34] - HM[2:34] - HN[0:32] + HM[0:32])
    metric = 1.0 + slope_x * slope_x + slope_y * slope_y
    top = (
        bend_xx * (1.0 + slope_y * slope_y) + bend_yy * (1.0 + slope_x * slope_x)
        - 2.0 * slope_x * slope_y * bend_xy
    )
    curv[...] = top / (metric * jnp.sqrt(metric))


def pinned(x):
    return pltpu.with_memory_space_constraint(x, pltpu.HBM)


def pass_kernel(*refs):
    n = (len(refs) - 1) // 2
    sources = [refs[0].at[:, 8:40, :]] + list(refs[1:n])
    moves = [pltpu.make_async_copy(sources[k], refs[n + k], refs[-1].at[k]) for k in range(n)]
    for c in moves:
        c.start()
    for c in moves:
        c.wait()


def body(fraction, velocity, centres, points, active_points, counts, rigid_start, mass, inertia):
    vmem, anywhere = pl.BlockSpec(memory_space=pltpu.VMEM), pl.BlockSpec(memory_space=pl.ANY)
    hbm = pl.BlockSpec(memory_space=pltpu.HBM)

    def f32(*shape):
        return jax.ShapeDtypeStruct(shape, F32)

    def room(*shape, dtype=F32):
        return pltpu.VMEM(shape, dtype)

    outs = (f32(16, 32, 128), f32(32, 128), f32(3, 128, 128), f32(6, 128))
    results = pl.pallas_call(
        brick_kernel,
        out_shape=(f32(16, 48, 128),) + outs[1:],
        in_specs=[hbm] * 3 + [pl.BlockSpec(memory_space=pltpu.SMEM)] + [hbm] * 5,
        out_specs=(vmem,) * 4,
        scratch_shapes=[
            pltpu.SMEM((3, 128), I32),
            room(128, 128, dtype=I32), room(128, 128, dtype=I32), room(6, 128), room(1, 128), room(1, 128),
            room(128, 128, dtype=I32), room(128, 128, dtype=I32), room(128, 128, dtype=I32),
            room(128, 128), room(128, 128), room(128, 128), room(3, 128, 128), room(24, 128, 128), room(128, 128),
            room(2, 3, 24, 48, 128), room(24, 48, 128),
            room(4, 48, 128), room(4, 48, 128), room(6, 48, 128), room(6, 48, 128), room(6, 48, 128),
            room(2, 4, 8, 128), room(2, 4, 8, 128), room(3, 2, 6, 8, 128), room(3, 2, 6, 8, 128),
            room(3, 3, 48, 128), room(3, 3, 48, 128), room(3, 40, 128), room(18, 40, 128),
            room(40, 128), room(40, 128), room(2, 2, 40, 128), room(40, 128), room(40, 128), room(40, 128),
            pltpu.SemaphoreType.DMA((8,)),
            pltpu.SemaphoreType.DMA((18,)), pltpu.SemaphoreType.DMA((18,)),
            pltpu.SemaphoreType.DMA((5,)), pltpu.SemaphoreType.DMA((5,)),
        ],
        compiler_params=pltpu.CompilerParams(
            collective_id=0, has_side_effects=True, vmem_limit_bytes=40 << 20
        ),
        name="brick",
    )(
        *(pinned(x) for x in (fraction, velocity, centres)), counts,
        *(pinned(x) for x in (points, active_points, rigid_start, mass.reshape(1, 128), inertia.reshape(1, 128))),
    )
    return pl.pallas_call(
        pass_kernel,
        out_shape=outs,
        in_specs=[anywhere] * 4,
        out_specs=(hbm,) * 4,
        scratch_shapes=[pltpu.SemaphoreType.DMA((4,))],
        compiler_params=pltpu.CompilerParams(vmem_limit_bytes=4 << 20),
        name="pass_on",
    )(*results)


def solution(mesh):
    bricks = ("gx", "gy", "gz")
    placed = (
        P("gz", "gx", "gy"), P(None, "gz", "gx", "gy"), P(None, bricks), P(bricks, None), P(bricks, None),
        P(bricks), P(None, bricks), P(bricks), P(bricks),
    )
    return jax.shard_map(
        body, mesh=mesh, in_specs=placed,
        out_specs=(P("gz", "gx", "gy"), P("gx", "gy"), P(None, bricks, None), P(None, bricks)),
        check_vma=False,
    )
```

```python
import jax
import jax.numpy as jnp
from jax import lax
from jax.experimental import pallas as pl
from jax.experimental.pallas import tpu as pltpu
from jax.sharding import PartitionSpec as P

MESH = pl.DeviceIdType.MESH
GROUP = 64
F32 = jnp.float32
I32 = jnp.int32

ACROSS = [(dx, dy) for dx in (-1, 0, 1) for dy in (-1, 0, 1) if dx or dy]


def lanes_of(shape):
    return lax.broadcasted_iota(I32, shape, len(shape) - 1)


def loop(steps, step, per=1):
    def some(g, _):
        for j in range(per):
            step(g * per + j, 0)
        return 0

    if steps == per:
        for k in range(steps):
            step(k, 0)
    else:
        lax.fori_loop(0, steps // per, some, 0)


def rows8(first):
    return pl.ds(first if isinstance(first, int) else pl.multiple_of(first, 8), 8)


def turn(x, by):
    by %= 128
    return pltpu.roll(x, by, x.ndim - 1) if by else x


def along(x, idx, axis):
    return jnp.take_along_axis(x, idx, axis=axis, mode="promise_in_bounds")


def cross(a, b):
    return [a[1] * b[2] - a[2] * b[1], a[2] * b[0] - a[0] * b[2], a[0] * b[1] - a[1] * b[0]]


def brick_kernel(
    frac, vel, cen_in, counts, points_in, active_in, start_in, mass_in, inertia_in,
    fout, curv, mult, motion,
    cen, points, active, rigid, mass, inertia, ED, ER, EC, WT, A, AT, SM, CB, RM, T,
    F, QU, QD, RQL, RQH, RV, PL, PR, RL, RR, PH, PV, SH, SQ, HB, HP, HY, HS, HN, HM,
    in_sem, send, recv, hsend, hrecv,
):
    gx, gy, gz = (lax.axis_index(a) for a in ("gx", "gy", "gz"))

    def place(dx, dy, dz):
        return (lax.rem(gx + dx + 16, 16), lax.rem(gy + dy + 8, 8), gz if dz == 0 else 1 - gz)

    everyone = [(dx, dy, dz) for dz in (0, 1) for dx, dy in ACROSS] + [(0, 0, 1)]
    own = [
        pltpu.make_async_copy(vel, T.at[0, :, 4:20, 8:40, :], in_sem.at[0]),
        pltpu.make_async_copy(frac, F.at[4:20, 8:40, :], in_sem.at[1]),
    ]
    for c in own:
        c.start()
    barrier = pltpu.get_barrier_semaphore()
    for off in everyone:
        pl.semaphore_signal(barrier, inc=1, device_id=place(*off), device_id_type=MESH)

    small = [
        pltpu.make_async_copy(src, dst, in_sem.at[2 + k])
        for k, (src, dst) in enumerate((
            (points_in, points), (active_in, active), (start_in, rigid), (mass_in, mass),
            (inertia_in, inertia), (cen_in, cen),
        ))
    ]
    for c in small:
        c.start()

    low = 12 * (1 - gz)
    copies = {}
    count = [0]

    def start(key, src, dst, off):
        k = count[0]
        count[0] += 1
        c = pltpu.make_async_remote_copy(
            src_ref=src, dst_ref=dst, send_sem=send.at[k], recv_sem=recv.at[k], device_id=place(*off),
            device_id_type=MESH,
        )
        c.start()
        copies[key] = c

    for c in own:
        c.wait()

    def layers(c, d):
        return T.at[0, c, d] if c < 3 else F.at[d]

    def pack_rows(g, _):
        for dd in range(4):
            for c in range(4):
                at = 12 * dd + 3 * c
                QU[g, at : at + 3, :] = layers(c, 4 + 4 * g + dd)[37:40, :]
                QD[g, at : at + 3, :] = layers(c, 4 + 4 * g + dd)[8:11, :]
        return 0

    loop(4, pack_rows, 2)
    pl.semaphore_wait(barrier, len(everyone))
    for dx, src, dst in ((1, QU, RQL), (-1, QD, RQH)):
        start((dx, 0, 0), src, dst.at[1:5], (dx, 0, 0))
        start((dx, 0, 1), src.at[3 * (1 - gz)], dst.at[5 * gz], (dx, 0, 1))

    start("z", vel.at[:, pl.ds(low, 4)], T.at[0, :, pl.ds(20 * gz, 4), 8:40, :], (0, 0, 1))
    start("zf", frac.at[pl.ds(low, 4)], F.at[pl.ds(20 * gz, 4), 8:40, :], (0, 0, 1))

    lane = lanes_of((8, 128))
    spot = lane // 8
    first = (lane % 8) < 4

    def pack_lanes(t, _):
        rows = rows8(8 + 8 * t)
        both = []
        for c in range(4):
            acc = None
            for d in range(16):
                v = turn(layers(c, 4 + d)[rows, :], 8 * d + 4)
                acc = v if d == 0 else jnp.where(spot == d, v, acc)
            both.append(acc)
        for h in range(2):
            a, b = both[2 * h], both[2 * h + 1]
            PL[h, t] = jnp.where(first, a, turn(b, 4))
            PR[h, t] = jnp.where(first, turn(a, -4), b)
        return 0

    loop(4, pack_lanes, 4)
    for dx in (0, 1, -1):
        ts, td = {0: (slice(0, 4), slice(1, 5)), 1: (3, 0), -1: (0, 5)}[dx]
        for dz in (0, 1):
            for dy, src, dst in ((1, PL, RL), (-1, PR, RR)):
                start((dx, dy, dz), src.at[:, ts], dst.at[2 * gz if dz else 1, :, td], (dx, dy, dz))

    RQL[5 * gz] = jnp.zeros((48, 128), F32)
    RQH[5 * gz] = jnp.zeros((48, 128), F32)
    RL[2 * gz] = jnp.zeros((2, 6, 8, 128), F32)
    RR[2 * gz] = jnp.zeros((2, 6, 8, 128), F32)
    blank = jnp.zeros((4, 32, 128), F32)
    for c in range(3):
        T[0, c, pl.ds(20 * gz, 4), 8:40, :] = blank
        T[1, c, pl.ds(20 * gz, 4), 8:40, :] = blank
    F[pl.ds(20 * gz, 4), 8:40, :] = blank

    def aside(x):
        return jnp.where(lanes_of(x.shape) < 64, turn(x, 60), turn(x, 68))

    def fill_aside(k, _):
        for c in range(3):
            T[1, c, 4 + k, 8:40, :] = aside(T[0, c, 4 + k, 8:40, :])
        return 0

    loop(16, fill_aside, 4)

    for c in small:
        c.wait()
    A[...] = jnp.zeros((128, 128), F32)
    A[0:6, :] = rigid[...]
    A[6:7, :] = mass[...]
    A[7:8, :] = inertia[...]
    AT[...] = A[...].T
    owned = counts[0]
    ones = jnp.ones((256, 128), jnp.bfloat16)

    def total(x):
        return jnp.dot(x.astype(jnp.bfloat16), ones[:128], preferred_element_type=F32)

    def prepare(k, _):
        base = pl.multiple_of(32 * k, 32)
        rows = pl.ds(base, 32)
        code = points[rows, :]
        ed = (code * 1338) >> 16
        rest = code - ed * 49
        er = (rest * 9363) >> 16
        ec = rest - er * 7
        ED[rows, :] = ed
        ER[rows, :] = er
        EC[rows, :] = ec
        alive = ((lax.broadcasted_iota(I32, (32, 128), 0) + base) < owned).astype(F32)
        w = active[rows, :].astype(F32) * alive
        WT[rows, :] = w
        e = [(x - 3).astype(F32) for x in (ed, er, ec)]
        we = [w * x for x in e]
        m0 = total(w)
        m1 = [total(x) for x in we]
        m2 = {(i, j): total(we[i] * e[j]) for i in range(3) for j in range(i, 3)}
        J = [m2[(1, 1)] + m2[(2, 2)], m2[(0, 0)] + m2[(2, 2)], m2[(0, 0)] + m2[(1, 1)]]
        columns = AT[rows, :]
        column = [jnp.broadcast_to(columns[:, c : c + 1], (32, 128)) for c in range(8)]
        for c, x in enumerate(column + [m0] + m1 + J + [m2[(0, 1)], m2[(0, 2)], m2[(1, 2)]]):
            CB[c, rows, :] = x
        force, torque = pull(column[0:3], column[3:6], m0, m1, J, m2[(0, 1)], m2[(0, 2)], m2[(1, 2)])
        for c, x in enumerate(force + torque):
            CB[18 + c, rows, :] = x
        return 0

    def pull(linear, angular, m0, m1, J, xy, xz, yz):
        turned = cross(angular, m1)
        force = [m0 * linear[c] + turned[c] for c in range(3)]
        lever = cross(m1, linear)
        torque = [
            lever[0] + (J[0] * angular[0] - xy * angular[1] - xz * angular[2]),
            lever[1] + (J[1] * angular[1] - xy * angular[0] - yz * angular[2]),
            lever[2] + (J[2] * angular[2] - xz * angular[0] - yz * angular[1]),
        ]
        return force, torque

    loop(4, prepare, 2)
    copies["z"].wait()
    copies["zf"].wait()

    def fill_aside_partner(k, _):
        for c in range(3):
            T[1, c, 20 * (1 - gz) + k, 8:40, :] = aside(T[0, c, 20 * (1 - gz) + k, 8:40, :])
        return 0

    loop(4, fill_aside_partner, 4)

    in_low, in_high = (gx > 0).astype(F32), (gx < 15).astype(F32)
    in_left, in_right = (gy > 0).astype(F32), (gy < 7).astype(F32)
    ranks = ((1, RQL, 5, in_low), (-1, RQH, 40, in_high))
    for dx, src, to, here in ranks:
        copies[(dx, 0, 0)].wait()
        copies[(dx, 0, 1)].wait()

        def unpack_rows(g, _):
            for dd in range(4):
                for c in range(4):
                    at = 12 * dd + 3 * c
                    layers(c, 4 * g + dd)[to : to + 3, :] = src[g, at : at + 3, :] * here
            return 0

        loop(6, unpack_rows, 2)

    for dx, src, to, here in ranks:
        def shift_rows(g, _):
            RV[g] = aside(src[g] * here)
            return 0

        def place_rows(g, _):
            for dd in range(4):
                for c in range(3):
                    at = 12 * dd + 3 * c
                    T[1, c, 4 * g + dd, to : to + 3, :] = RV[g, at : at + 3, :]
            return 0

        loop(6, shift_rows, 6)
        loop(6, place_rows, 2)

    for dy in (1, -1):
        for dx in (0, 1, -1):
            copies[(dx, dy, 0)].wait()
            copies[(dx, dy, 1)].wait()

    def merge(t, _):
        rows = rows8(8 * t)
        here = jnp.where(t == 0, in_low, jnp.where(t == 5, in_high, 1.0))
        left, right = in_left * here, in_right * here
        for lev in range(3):
            for c in range(4):
                a, b = RL[lev, c // 2, t] * left, RR[lev, c // 2, t] * right
                if c > 0:
                    PH[c - 1, lev, rows, :] = (
                        jnp.where(first, turn(a, -4), b) if c % 2 else jnp.where(first, a, turn(b, 4))
                    )
                if c < 3:
                    PV[c, lev, rows, :] = (
                        jnp.where(first, turn(b, -4), a) if c % 2 else jnp.where(first, b, turn(a, 4))
                    )
        return 0

    loop(6, merge, 6)

    wide = lanes_of((40, 128))
    head, tail = wide == 0, wide == 127

    def flux_of(speed, below, above):
        return jnp.maximum(speed, 0.0) * below + jnp.minimum(speed, 0.0) * above

    def swept(q, flux_low, flux_high, speed_low, speed_high):
        return q - (flux_high - flux_low) + q * (speed_high - speed_low)

    def sweep_of(q, u):
        lo, hi = 0.5 * (u[0] + u[1]), 0.5 * (u[1] + u[2])
        return swept(q[1], flux_of(lo, q[0], q[1]), flux_of(hi, q[1], q[2]), lo, hi)

    for lev in range(3):
        SH[lev] = sweep_of(
            [PH[2, lev, 6 + o : 46 + o, :] for o in range(3)], [PH[0, lev, 6 + o : 46 + o, :] for o in range(3)]
        )

    def sweep_xy(k, _):
        d = 3 + k
        q = sweep_of(
            [F[d, 6 + o : 46 + o, :] for o in range(3)], [T[0, 1, d, 6 + o : 46 + o, :] for o in range(3)]
        )
        u = T[0, 2, d, 7:47, :]
        lev = jnp.where(k == 0, 0, jnp.where(k == 17, 2, 1))
        by = 124 - 8 * ((k + 15) % 16)
        qh, uh = pltpu.roll(SH[lev], by, 1), pltpu.roll(PH[1, lev, 7:47, :], by, 1)
        ql, ul = turn(jnp.where(tail, qh, q), 1), turn(jnp.where(tail, uh, u), 1)
        qr, ur = turn(jnp.where(head, qh, q), -1), turn(jnp.where(head, uh, u), -1)
        SQ[k] = sweep_of([ql, q, qr], [ul, u, ur])
        return 0

    loop(18, sweep_xy, 6)

    def sweep_z(k, carry):
        total_height, q, u, speed, flux = carry
        above, u_above = SQ[k + 2], T[0, 0, 5 + k, 7:47, :]
        speed_above = 0.5 * (u + u_above)
        flux_above = flux_of(speed_above, q, above)
        new = swept(q, flux, flux_above, speed, speed_above)
        fout[k, 7:47, :] = new
        return total_height + new, above, u_above, speed_above, flux_above

    u0, u1 = T[0, 0, 3, 7:47, :], T[0, 0, 4, 7:47, :]
    speed0 = 0.5 * (u0 + u1)
    def sweep_z_some(g, carry):
        for j in range(4):
            carry = sweep_z(g * 4 + j, carry)
        return carry

    HB[...] = lax.fori_loop(
        0, 4, sweep_z_some, (jnp.zeros((40, 128), F32), SQ[1], u1, speed0, flux_of(speed0, SQ[0], SQ[1]))
    )[0]

    heights = []
    for j, (dy, dz) in enumerate([(1, 1), (-1, 1), (1, 0), (-1, 0), (0, 1)]):
        c = pltpu.make_async_remote_copy(
            src_ref=HB, dst_ref=HY.at[dz, (dy < 0) * 1] if dy else HP, send_sem=hsend.at[j], recv_sem=hrecv.at[j],
            device_id=place(0, dy, dz), device_id_type=MESH,
        )
        c.start()
        heights.append(c)

    joint = (lane >= 60) & (lane < 68)

    def unpack_lanes(t, _):
        rows = rows8(8 * t)
        for c in range(3):
            for lev, near in ((0, range(13, 16)), (1, range(16)), (2, range(3))):
                v = PV[c, lev, rows, :]
                for d in near:
                    at = 4 + 16 * (lev - 1) + d
                    pltpu.store(T.at[1, c, at, rows, :], turn(v, 60 - 8 * d), mask=joint)
        return 0

    loop(6, unpack_lanes, 6)

    row8 = lax.broadcasted_iota(I32, (8, 128), 0)

    def sample(g, _):
        base = pl.multiple_of(g * GROUP, GROUP)
        tiles = [[None] * (GROUP // 8) for _ in range(3)]
        for s in range(GROUP):
            q = base + s
            d0 = jnp.clip(cen[0, q] - 2, 1, 16)
            r0 = jnp.clip(cen[1, q] + 2, 5, 36)
            jc = cen[2, q] - 3
            at_left, at_right = (jc < 3).astype(I32), (jc > 124).astype(I32)
            side = at_left + at_right
            first_lane = jc - 3 + 68 * (at_left - at_right)
            e_d = jnp.broadcast_to(ED[pl.ds(q, 1), :], (8, 128))
            e_r = jnp.broadcast_to(ER[pl.ds(q, 1), :], (8, 128))
            idx = (jnp.broadcast_to(EC[pl.ds(q, 1), :], (8, 128)) + first_lane) & 127
            picks = [e_d == k for k in range(1, 7)]
            for c in range(3):
                acc = None
                for k in range(7):
                    v = along(T[side, c, d0 + k, pl.ds(r0, 8), :], idx, 1)
                    acc = v if k == 0 else jnp.where(picks[k - 1], v, acc)
                res = along(acc, e_r, 0)
                old = tiles[c][s // 8]
                tiles[c][s // 8] = res if s % 8 == 0 else jnp.where(row8 == s % 8, res, old)
        for c in range(3):
            SM[c, pl.ds(base, GROUP), :] = jnp.concatenate(tiles[c], axis=0)
        return 0

    loop(128 // GROUP, sample, 1)

    def total_of(x):
        high = x.astype(jnp.bfloat16)
        rest = (x - high.astype(F32)).astype(jnp.bfloat16)
        return jnp.dot(jnp.concatenate([high, rest], axis=1), ones, preferred_element_type=F32)

    def iterate(k, _):
        rows = pl.ds(pl.multiple_of(32 * k, 32), 32)
        s = [SM[c, rows, :] for c in range(3)]
        w = WT[rows, :]
        e = [(x[rows, :] - 3).astype(F32) for x in (ED, ER, EC)]
        ws = [w * x for x in s]
        S = [total_of(x) for x in ws]
        Q = [total_of(x) for x in cross(e, ws)]
        n = [CB[c, rows, :] for c in range(24)]
        linear, angular, force, torque = n[0:3], n[3:6], n[18:21], n[21:24]
        linear1 = [linear[c] + n[6] * (S[c] - force[c]) for c in range(3)]
        angular1 = [angular[c] + n[7] * (Q[c] - torque[c]) for c in range(3)]
        force1, torque1 = pull(linear1, angular1, n[8], n[9:12], n[12:15], n[15], n[16], n[17])
        last = [linear[c] + n[6] * (1.5 * S[c] - 0.5 * force[c] - force1[c]) for c in range(3)]
        last += [angular[c] + n[7] * (1.5 * Q[c] - 0.5 * torque[c] - torque1[c]) for c in range(3)]
        both = [0.5 * linear[c] + linear1[c] for c in range(3)]
        spin = cross([0.5 * angular[c] + angular1[c] for c in range(3)], e)
        for c in range(3):
            mult[c, rows, :] = 1.5 * ws[c] - w * (both[c] + spin[c])
        lanes = lanes_of((32, 128))
        out = jnp.zeros((32, 128), F32)
        for c in range(6):
            out = jnp.where(lanes == c, last[c], out)
        alive = ((lax.broadcasted_iota(I32, (32, 128), 0) + 32 * k) < owned).astype(F32)
        RM[rows, :] = out * alive
        return 0

    loop(4, iterate, 4)
    motion[...] = RM[...].T[0:6, :]

    for c in heights:
        c.wait()

    row = lax.broadcasted_iota(I32, (40, 128), 0)
    inside = jnp.where(row == 0, in_low, jnp.where(row == 33, in_high, 1.0))
    h = (HB[...] + HP[...]) * inside
    hh = jnp.where(wide >= 64, (HY[0, 0] + HY[1, 0]) * in_left, (HY[0, 1] + HY[1, 1]) * in_right) * inside
    HS[...] = h
    HN[...] = turn(jnp.where(head, hh, h), -1)
    HM[...] = turn(jnp.where(tail, hh, h), 1)
    middle, east, west = HS[1:33], HS[2:34], HS[0:32]
    north, south = HN[1:33], HM[1:33]
    slope_x, slope_y = 0.5 * (east - west), 0.5 * (north - south)
    bend_xx = east - 2.0 * middle + west
    bend_yy = north - 2.0 * middle + south
    bend_xy = 0.25 * (HN[2:34] - HM[2:34] - HN[0:32] + HM[0:32])
    metric = 1.0 + slope_x * slope_x + slope_y * slope_y
    top = (
        bend_xx * (1.0 + slope_y * slope_y) + bend_yy * (1.0 + slope_x * slope_x)
        - 2.0 * slope_x * slope_y * bend_xy
    )
    curv[...] = top / (metric * jnp.sqrt(metric))


def pinned(x):
    return pltpu.with_memory_space_constraint(x, pltpu.HBM)


def pass_kernel(*refs):
    n = (len(refs) - 1) // 2
    sources = [refs[0].at[:, 8:40, :]] + list(refs[1:n])
    moves = [pltpu.make_async_copy(sources[k], refs[n + k], refs[-1].at[k]) for k in range(n)]
    for c in moves:
        c.start()
    for c in moves:
        c.wait()


def body(fraction, velocity, centres, points, active_points, counts, rigid_start, mass, inertia):
    vmem, anywhere = pl.BlockSpec(memory_space=pltpu.VMEM), pl.BlockSpec(memory_space=pl.ANY)
    hbm = pl.BlockSpec(memory_space=pltpu.HBM)

    def f32(*shape):
        return jax.ShapeDtypeStruct(shape, F32)

    def room(*shape, dtype=F32):
        return pltpu.VMEM(shape, dtype)

    outs = (f32(16, 32, 128), f32(32, 128), f32(3, 128, 128), f32(6, 128))
    results = pl.pallas_call(
        brick_kernel,
        out_shape=(f32(16, 48, 128),) + outs[1:],
        in_specs=[hbm] * 3 + [pl.BlockSpec(memory_space=pltpu.SMEM)] + [hbm] * 5,
        out_specs=(vmem,) * 4,
        scratch_shapes=[
            pltpu.SMEM((3, 128), I32),
            room(128, 128, dtype=I32), room(128, 128, dtype=I32), room(6, 128), room(1, 128), room(1, 128),
            room(128, 128, dtype=I32), room(128, 128, dtype=I32), room(128, 128, dtype=I32),
            room(128, 128), room(128, 128), room(128, 128), room(3, 128, 128), room(24, 128, 128), room(128, 128),
            room(2, 3, 24, 48, 128), room(24, 48, 128),
            room(4, 48, 128), room(4, 48, 128), room(6, 48, 128), room(6, 48, 128), room(6, 48, 128),
            room(2, 4, 8, 128), room(2, 4, 8, 128), room(3, 2, 6, 8, 128), room(3, 2, 6, 8, 128),
            room(3, 3, 48, 128), room(3, 3, 48, 128), room(3, 40, 128), room(18, 40, 128),
            room(40, 128), room(40, 128), room(2, 2, 40, 128), room(40, 128), room(40, 128), room(40, 128),
            pltpu.SemaphoreType.DMA((8,)),
            pltpu.SemaphoreType.DMA((18,)), pltpu.SemaphoreType.DMA((18,)),
            pltpu.SemaphoreType.DMA((5,)), pltpu.SemaphoreType.DMA((5,)),
        ],
        compiler_params=pltpu.CompilerParams(
            collective_id=0, has_side_effects=True, vmem_limit_bytes=40 << 20
        ),
        name="brick",
    )(
        *(pinned(x) for x in (fraction, velocity, centres)), counts,
        *(pinned(x) for x in (points, active_points, rigid_start, mass.reshape(1, 128), inertia.reshape(1, 128))),
    )
    return pl.pallas_call(
        pass_kernel,
        out_shape=outs,
        in_specs=[anywhere] * 4,
        out_specs=(hbm,) * 4,
        scratch_shapes=[pltpu.SemaphoreType.DMA((4,))],
        compiler_params=pltpu.CompilerParams(vmem_limit_bytes=4 << 20),
        name="pass_on",
    )(*results)


def solution(mesh):
    bricks = ("gx", "gy", "gz")
    placed = (
        P("gz", "gx", "gy"), P(None, "gz", "gx", "gy"), P(None, bricks), P(bricks, None), P(bricks, None),
        P(bricks), P(None, bricks), P(bricks), P(bricks),
    )
    return jax.shard_map(
        body, mesh=mesh, in_specs=placed,
        out_specs=(P("gz", "gx", "gy"), P("gx", "gy"), P(None, bricks, None), P(None, bricks)),
        check_vma=False,
    )
```

```python
import jax
import jax.numpy as jnp
from jax import lax
from jax.experimental import pallas as pl
from jax.experimental.pallas import tpu as pltpu
from jax.sharding import PartitionSpec as P

MESH = pl.DeviceIdType.MESH
GROUP = 128
F32 = jnp.float32
I32 = jnp.int32

ACROSS = [(dx, dy) for dx in (-1, 0, 1) for dy in (-1, 0, 1) if dx or dy]


def lanes_of(shape):
    return lax.broadcasted_iota(I32, shape, len(shape) - 1)


def loop(steps, step, per=1):
    def some(g, _):
        for j in range(per):
            step(g * per + j, 0)
        return 0

    if steps == per:
        for k in range(steps):
            step(k, 0)
    else:
        lax.fori_loop(0, steps // per, some, 0)


def rows8(first):
    return pl.ds(first if isinstance(first, int) else pl.multiple_of(first, 8), 8)


def turn(x, by):
    by %= 128
    return pltpu.roll(x, by, x.ndim - 1) if by else x


def along(x, idx, axis):
    return jnp.take_along_axis(x, idx, axis=axis, mode="promise_in_bounds")


def cross(a, b):
    return [a[1] * b[2] - a[2] * b[1], a[2] * b[0] - a[0] * b[2], a[0] * b[1] - a[1] * b[0]]


def brick_kernel(
    frac, vel, cen_in, counts, points_in, active_in, start_in, mass_in, inertia_in,
    fout, curv, mult, motion,
    cen, points, active, rigid, mass, inertia, ED, ER, EC, WT, A, AT, SM, CB, RM, T,
    F, QU, QD, RQL, RQH, RV, PL, PR, RL, RR, PH, PV, SH, SQ, HB, HP, HY, HS, HN, HM,
    in_sem, send, recv, hsend, hrecv,
):
    gx, gy, gz = (lax.axis_index(a) for a in ("gx", "gy", "gz"))

    def place(dx, dy, dz):
        return (lax.rem(gx + dx + 16, 16), lax.rem(gy + dy + 8, 8), gz if dz == 0 else 1 - gz)

    everyone = [(dx, dy, dz) for dz in (0, 1) for dx, dy in ACROSS] + [(0, 0, 1)]
    own = [
        pltpu.make_async_copy(vel, T.at[0, :, 4:20, 8:40, :], in_sem.at[0]),
        pltpu.make_async_copy(frac, F.at[4:20, 8:40, :], in_sem.at[1]),
    ]
    for c in own:
        c.start()
    barrier = pltpu.get_barrier_semaphore()
    for off in everyone:
        pl.semaphore_signal(barrier, inc=1, device_id=place(*off), device_id_type=MESH)

    small = [
        pltpu.make_async_copy(src, dst, in_sem.at[2 + k])
        for k, (src, dst) in enumerate((
            (points_in, points), (active_in, active), (start_in, rigid), (mass_in, mass),
            (inertia_in, inertia), (cen_in, cen),
        ))
    ]
    for c in small:
        c.start()

    low = 12 * (1 - gz)
    copies = {}
    count = [0]

    def start(key, src, dst, off):
        k = count[0]
        count[0] += 1
        c = pltpu.make_async_remote_copy(
            src_ref=src, dst_ref=dst, send_sem=send.at[k], recv_sem=recv.at[k], device_id=place(*off),
            device_id_type=MESH,
        )
        c.start()
        copies[key] = c

    for c in own:
        c.wait()

    def layers(c, d):
        return T.at[0, c, d] if c < 3 else F.at[d]

    def pack_rows(g, _):
        for dd in range(4):
            for c in range(4):
                at = 12 * dd + 3 * c
                QU[g, at : at + 3, :] = layers(c, 4 + 4 * g + dd)[37:40, :]
                QD[g, at : at + 3, :] = layers(c, 4 + 4 * g + dd)[8:11, :]
        return 0

    loop(4, pack_rows, 2)
    pl.semaphore_wait(barrier, len(everyone))
    for dx, src, dst in ((1, QU, RQL), (-1, QD, RQH)):
        start((dx, 0, 0), src, dst.at[1:5], (dx, 0, 0))
        start((dx, 0, 1), src.at[3 * (1 - gz)], dst.at[5 * gz], (dx, 0, 1))

    start("z", vel.at[:, pl.ds(low, 4)], T.at[0, :, pl.ds(20 * gz, 4), 8:40, :], (0, 0, 1))
    start("zf", frac.at[pl.ds(low, 4)], F.at[pl.ds(20 * gz, 4), 8:40, :], (0, 0, 1))

    lane = lanes_of((8, 128))
    spot = lane // 8
    first = (lane % 8) < 4

    def pack_lanes(t, _):
        rows = rows8(8 + 8 * t)
        both = []
        for c in range(4):
            acc = None
            for d in range(16):
                v = turn(layers(c, 4 + d)[rows, :], 8 * d + 4)
                acc = v if d == 0 else jnp.where(spot == d, v, acc)
            both.append(acc)
        for h in range(2):
            a, b = both[2 * h], both[2 * h + 1]
            PL[h, t] = jnp.where(first, a, turn(b, 4))
            PR[h, t] = jnp.where(first, turn(a, -4), b)
        return 0

    loop(4, pack_lanes, 4)
    for dx in (0, 1, -1):
        ts, td = {0: (slice(0, 4), slice(1, 5)), 1: (3, 0), -1: (0, 5)}[dx]
        for dz in (0, 1):
            for dy, src, dst in ((1, PL, RL), (-1, PR, RR)):
                start((dx, dy, dz), src.at[:, ts], dst.at[2 * gz if dz else 1, :, td], (dx, dy, dz))

    RQL[5 * gz] = jnp.zeros((48, 128), F32)
    RQH[5 * gz] = jnp.zeros((48, 128), F32)
    RL[2 * gz] = jnp.zeros((2, 6, 8, 128), F32)
    RR[2 * gz] = jnp.zeros((2, 6, 8, 128), F32)
    blank = jnp.zeros((4, 32, 128), F32)
    for c in range(3):
        T[0, c, pl.ds(20 * gz, 4), 8:40, :] = blank
        T[1, c, pl.ds(20 * gz, 4), 8:40, :] = blank
    F[pl.ds(20 * gz, 4), 8:40, :] = blank

    def aside(x):
        return jnp.where(lanes_of(x.shape) < 64, turn(x, 60), turn(x, 68))

    def fill_aside(k, _):
        for c in range(3):
            T[1, c, 4 + k, 8:40, :] = aside(T[0, c, 4 + k, 8:40, :])
        return 0

    loop(16, fill_aside, 4)

    for c in small:
        c.wait()
    A[...] = jnp.zeros((128, 128), F32)
    A[0:6, :] = rigid[...]
    A[6:7, :] = mass[...]
    A[7:8, :] = inertia[...]
    AT[...] = A[...].T
    owned = counts[0]
    ones = jnp.ones((256, 128), jnp.bfloat16)

    def total(x):
        return jnp.dot(x.astype(jnp.bfloat16), ones[:128], preferred_element_type=F32)

    def prepare(k, _):
        base = pl.multiple_of(32 * k, 32)
        rows = pl.ds(base, 32)
        code = points[rows, :]
        ed = (code * 1338) >> 16
        rest = code - ed * 49
        er = (rest * 9363) >> 16
        ec = rest - er * 7
        ED[rows, :] = ed
        ER[rows, :] = er
        EC[rows, :] = ec
        alive = ((lax.broadcasted_iota(I32, (32, 128), 0) + base) < owned).astype(F32)
        w = active[rows, :].astype(F32) * alive
        WT[rows, :] = w
        e = [(x - 3).astype(F32) for x in (ed, er, ec)]
        we = [w * x for x in e]
        m0 = total(w)
        m1 = [total(x) for x in we]
        m2 = {(i, j): total(we[i] * e[j]) for i in range(3) for j in range(i, 3)}
        J = [m2[(1, 1)] + m2[(2, 2)], m2[(0, 0)] + m2[(2, 2)], m2[(0, 0)] + m2[(1, 1)]]
        columns = AT[rows, :]
        column = [jnp.broadcast_to(columns[:, c : c + 1], (32, 128)) for c in range(8)]
        for c, x in enumerate(column + [m0] + m1 + J + [m2[(0, 1)], m2[(0, 2)], m2[(1, 2)]]):
            CB[c, rows, :] = x
        force, torque = pull(column[0:3], column[3:6], m0, m1, J, m2[(0, 1)], m2[(0, 2)], m2[(1, 2)])
        for c, x in enumerate(force + torque):
            CB[18 + c, rows, :] = x
        return 0

    def pull(linear, angular, m0, m1, J, xy, xz, yz):
        turned = cross(angular, m1)
        force = [m0 * linear[c] + turned[c] for c in range(3)]
        lever = cross(m1, linear)
        torque = [
            lever[0] + (J[0] * angular[0] - xy * angular[1] - xz * angular[2]),
            lever[1] + (J[1] * angular[1] - xy * angular[0] - yz * angular[2]),
            lever[2] + (J[2] * angular[2] - xz * angular[0] - yz * angular[1]),
        ]
        return force, torque

    loop(4, prepare, 2)
    copies["z"].wait()
    copies["zf"].wait()

    def fill_aside_partner(k, _):
        for c in range(3):
            T[1, c, 20 * (1 - gz) + k, 8:40, :] = aside(T[0, c, 20 * (1 - gz) + k, 8:40, :])
        return 0

    loop(4, fill_aside_partner, 4)

    in_low, in_high = (gx > 0).astype(F32), (gx < 15).astype(F32)
    in_left, in_right = (gy > 0).astype(F32), (gy < 7).astype(F32)
    ranks = ((1, RQL, 5, in_low), (-1, RQH, 40, in_high))
    for dx, src, to, here in ranks:
        copies[(dx, 0, 0)].wait()
        copies[(dx, 0, 1)].wait()

        def unpack_rows(g, _):
            for dd in range(4):
                for c in range(4):
                    at = 12 * dd + 3 * c
                    layers(c, 4 * g + dd)[to : to + 3, :] = src[g, at : at + 3, :] * here
            return 0

        loop(6, unpack_rows, 2)

    for dx, src, to, here in ranks:
        def shift_rows(g, _):
            RV[g] = aside(src[g] * here)
            return 0

        def place_rows(g, _):
            for dd in range(4):
                for c in range(3):
                    at = 12 * dd + 3 * c
                    T[1, c, 4 * g + dd, to : to + 3, :] = RV[g, at : at + 3, :]
            return 0

        loop(6, shift_rows, 6)
        loop(6, place_rows, 2)

    for dy in (1, -1):
        for dx in (0, 1, -1):
            copies[(dx, dy, 0)].wait()
            copies[(dx, dy, 1)].wait()

    def merge(t, _):
        rows = rows8(8 * t)
        here = jnp.where(t == 0, in_low, jnp.where(t == 5, in_high, 1.0))
        left, right = in_left * here, in_right * here
        for lev in range(3):
            for c in range(4):
                a, b = RL[lev, c // 2, t] * left, RR[lev, c // 2, t] * right
                if c > 0:
                    PH[c - 1, lev, rows, :] = (
                        jnp.where(first, turn(a, -4), b) if c % 2 else jnp.where(first, a, turn(b, 4))
                    )
                if c < 3:
                    PV[c, lev, rows, :] = (
                        jnp.where(first, turn(b, -4), a) if c % 2 else jnp.where(first, b, turn(a, 4))
                    )
        return 0

    loop(6, merge, 6)

    wide = lanes_of((40, 128))
    head, tail = wide == 0, wide == 127

    def flux_of(speed, below, above):
        return jnp.maximum(speed, 0.0) * below + jnp.minimum(speed, 0.0) * above

    def swept(q, flux_low, flux_high, speed_low, speed_high):
        return q - (flux_high - flux_low) + q * (speed_high - speed_low)

    def sweep_of(q, u):
        lo, hi = 0.5 * (u[0] + u[1]), 0.5 * (u[1] + u[2])
        return swept(q[1], flux_of(lo, q[0], q[1]), flux_of(hi, q[1], q[2]), lo, hi)

    for lev in range(3):
        SH[lev] = sweep_of(
            [PH[2, lev, 6 + o : 46 + o, :] for o in range(3)], [PH[0, lev, 6 + o : 46 + o, :] for o in range(3)]
        )

    def sweep_xy(k, _):
        d = 3 + k
        q = sweep_of(
            [F[d, 6 + o : 46 + o, :] for o in range(3)], [T[0, 1, d, 6 + o : 46 + o, :] for o in range(3)]
        )
        u = T[0, 2, d, 7:47, :]
        lev = jnp.where(k == 0, 0, jnp.where(k == 17, 2, 1))
        by = 124 - 8 * ((k + 15) % 16)
        qh, uh = pltpu.roll(SH[lev], by, 1), pltpu.roll(PH[1, lev, 7:47, :], by, 1)
        ql, ul = turn(jnp.where(tail, qh, q), 1), turn(jnp.where(tail, uh, u), 1)
        qr, ur = turn(jnp.where(head, qh, q), -1), turn(jnp.where(head, uh, u), -1)
        SQ[k] = sweep_of([ql, q, qr], [ul, u, ur])
        return 0

    loop(18, sweep_xy, 6)

    def sweep_z(k, carry):
        total_height, q, u, speed, flux = carry
        above, u_above = SQ[k + 2], T[0, 0, 5 + k, 7:47, :]
        speed_above = 0.5 * (u + u_above)
        flux_above = flux_of(speed_above, q, above)
        new = swept(q, flux, flux_above, speed, speed_above)
        fout[k, 7:47, :] = new
        return total_height + new, above, u_above, speed_above, flux_above

    u0, u1 = T[0, 0, 3, 7:47, :], T[0, 0, 4, 7:47, :]
    speed0 = 0.5 * (u0 + u1)
    def sweep_z_some(g, carry):
        for j in range(4):
            carry = sweep_z(g * 4 + j, carry)
        return carry

    HB[...] = lax.fori_loop(
        0, 4, sweep_z_some, (jnp.zeros((40, 128), F32), SQ[1], u1, speed0, flux_of(speed0, SQ[0], SQ[1]))
    )[0]

    heights = []
    for j, (dy, dz) in enumerate([(1, 1), (-1, 1), (1, 0), (-1, 0), (0, 1)]):
        c = pltpu.make_async_remote_copy(
            src_ref=HB, dst_ref=HY.at[dz, (dy < 0) * 1] if dy else HP, send_sem=hsend.at[j], recv_sem=hrecv.at[j],
            device_id=place(0, dy, dz), device_id_type=MESH,
        )
        c.start()
        heights.append(c)

    joint = (lane >= 60) & (lane < 68)

    def unpack_lanes(t, _):
        rows = rows8(8 * t)
        for c in range(3):
            for lev, near in ((0, range(13, 16)), (1, range(16)), (2, range(3))):
                v = PV[c, lev, rows, :]
                for d in near:
                    at = 4 + 16 * (lev - 1) + d
                    pltpu.store(T.at[1, c, at, rows, :], turn(v, 60 - 8 * d), mask=joint)
        return 0

    loop(6, unpack_lanes, 6)

    row8 = lax.broadcasted_iota(I32, (8, 128), 0)

    def sample(g, _):
        base = pl.multiple_of(g * GROUP, GROUP)
        tiles = [[None] * (GROUP // 8) for _ in range(3)]
        for s in range(GROUP):
            q = base + s
            d0 = jnp.clip(cen[0, q] - 2, 1, 16)
            r0 = jnp.clip(cen[1, q] + 2, 5, 36)
            jc = cen[2, q] - 3
            at_left, at_right = (jc < 3).astype(I32), (jc > 124).astype(I32)
            side = at_left + at_right
            first_lane = jc - 3 + 68 * (at_left - at_right)
            e_d = jnp.broadcast_to(ED[pl.ds(q, 1), :], (8, 128))
            e_r = jnp.broadcast_to(ER[pl.ds(q, 1), :], (8, 128))
            idx = (jnp.broadcast_to(EC[pl.ds(q, 1), :], (8, 128)) + first_lane) & 127
            picks = [e_d == k for k in range(1, 7)]
            for c in range(3):
                acc = None
                for k in range(7):
                    v = along(T[side, c, d0 + k, pl.ds(r0, 8), :], idx, 1)
                    acc = v if k == 0 else jnp.where(picks[k - 1], v, acc)
                res = along(acc, e_r, 0)
                old = tiles[c][s // 8]
                tiles[c][s // 8] = res if s % 8 == 0 else jnp.where(row8 == s % 8, res, old)
        for c in range(3):
            SM[c, pl.ds(base, GROUP), :] = jnp.concatenate(tiles[c], axis=0)
        return 0

    loop(128 // GROUP, sample, 1)

    def total_of(x):
        high = x.astype(jnp.bfloat16)
        rest = (x - high.astype(F32)).astype(jnp.bfloat16)
        return jnp.dot(jnp.concatenate([high, rest], axis=1), ones, preferred_element_type=F32)

    def iterate(k, _):
        rows = pl.ds(pl.multiple_of(32 * k, 32), 32)
        s = [SM[c, rows, :] for c in range(3)]
        w = WT[rows, :]
        e = [(x[rows, :] - 3).astype(F32) for x in (ED, ER, EC)]
        ws = [w * x for x in s]
        S = [total_of(x) for x in ws]
        Q = [total_of(x) for x in cross(e, ws)]
        n = [CB[c, rows, :] for c in range(24)]
        linear, angular, force, torque = n[0:3], n[3:6], n[18:21], n[21:24]
        linear1 = [linear[c] + n[6] * (S[c] - force[c]) for c in range(3)]
        angular1 = [angular[c] + n[7] * (Q[c] - torque[c]) for c in range(3)]
        force1, torque1 = pull(linear1, angular1, n[8], n[9:12], n[12:15], n[15], n[16], n[17])
        last = [linear[c] + n[6] * (1.5 * S[c] - 0.5 * force[c] - force1[c]) for c in range(3)]
        last += [angular[c] + n[7] * (1.5 * Q[c] - 0.5 * torque[c] - torque1[c]) for c in range(3)]
        both = [0.5 * linear[c] + linear1[c] for c in range(3)]
        spin = cross([0.5 * angular[c] + angular1[c] for c in range(3)], e)
        for c in range(3):
            mult[c, rows, :] = 1.5 * ws[c] - w * (both[c] + spin[c])
        lanes = lanes_of((32, 128))
        out = jnp.zeros((32, 128), F32)
        for c in range(6):
            out = jnp.where(lanes == c, last[c], out)
        alive = ((lax.broadcasted_iota(I32, (32, 128), 0) + 32 * k) < owned).astype(F32)
        RM[rows, :] = out * alive
        return 0

    loop(4, iterate, 4)
    motion[...] = RM[...].T[0:6, :]

    for c in heights:
        c.wait()

    row = lax.broadcasted_iota(I32, (40, 128), 0)
    inside = jnp.where(row == 0, in_low, jnp.where(row == 33, in_high, 1.0))
    h = (HB[...] + HP[...]) * inside
    hh = jnp.where(wide >= 64, (HY[0, 0] + HY[1, 0]) * in_left, (HY[0, 1] + HY[1, 1]) * in_right) * inside
    HS[...] = h
    HN[...] = turn(jnp.where(head, hh, h), -1)
    HM[...] = turn(jnp.where(tail, hh, h), 1)
    middle, east, west = HS[1:33], HS[2:34], HS[0:32]
    north, south = HN[1:33], HM[1:33]
    slope_x, slope_y = 0.5 * (east - west), 0.5 * (north - south)
    bend_xx = east - 2.0 * middle + west
    bend_yy = north - 2.0 * middle + south
    bend_xy = 0.25 * (HN[2:34] - HM[2:34] - HN[0:32] + HM[0:32])
    metric = 1.0 + slope_x * slope_x + slope_y * slope_y
    top = (
        bend_xx * (1.0 + slope_y * slope_y) + bend_yy * (1.0 + slope_x * slope_x)
        - 2.0 * slope_x * slope_y * bend_xy
    )
    curv[...] = top / (metric * jnp.sqrt(metric))


def pinned(x):
    return pltpu.with_memory_space_constraint(x, pltpu.HBM)


def pass_kernel(*refs):
    n = (len(refs) - 1) // 2
    sources = [refs[0].at[:, 8:40, :]] + list(refs[1:n])
    moves = [pltpu.make_async_copy(sources[k], refs[n + k], refs[-1].at[k]) for k in range(n)]
    for c in moves:
        c.start()
    for c in moves:
        c.wait()


def body(fraction, velocity, centres, points, active_points, counts, rigid_start, mass, inertia):
    vmem, anywhere = pl.BlockSpec(memory_space=pltpu.VMEM), pl.BlockSpec(memory_space=pl.ANY)
    hbm = pl.BlockSpec(memory_space=pltpu.HBM)

    def f32(*shape):
        return jax.ShapeDtypeStruct(shape, F32)

    def room(*shape, dtype=F32):
        return pltpu.VMEM(shape, dtype)

    outs = (f32(16, 32, 128), f32(32, 128), f32(3, 128, 128), f32(6, 128))
    results = pl.pallas_call(
        brick_kernel,
        out_shape=(f32(16, 48, 128),) + outs[1:],
        in_specs=[hbm] * 3 + [pl.BlockSpec(memory_space=pltpu.SMEM)] + [hbm] * 5,
        out_specs=(vmem,) * 4,
        scratch_shapes=[
            pltpu.SMEM((3, 128), I32),
            room(128, 128, dtype=I32), room(128, 128, dtype=I32), room(6, 128), room(1, 128), room(1, 128),
            room(128, 128, dtype=I32), room(128, 128, dtype=I32), room(128, 128, dtype=I32),
            room(128, 128), room(128, 128), room(128, 128), room(3, 128, 128), room(24, 128, 128), room(128, 128),
            room(2, 3, 24, 48, 128), room(24, 48, 128),
            room(4, 48, 128), room(4, 48, 128), room(6, 48, 128), room(6, 48, 128), room(6, 48, 128),
            room(2, 4, 8, 128), room(2, 4, 8, 128), room(3, 2, 6, 8, 128), room(3, 2, 6, 8, 128),
            room(3, 3, 48, 128), room(3, 3, 48, 128), room(3, 40, 128), room(18, 40, 128),
            room(40, 128), room(40, 128), room(2, 2, 40, 128), room(40, 128), room(40, 128), room(40, 128),
            pltpu.SemaphoreType.DMA((8,)),
            pltpu.SemaphoreType.DMA((18,)), pltpu.SemaphoreType.DMA((18,)),
            pltpu.SemaphoreType.DMA((5,)), pltpu.SemaphoreType.DMA((5,)),
        ],
        compiler_params=pltpu.CompilerParams(
            collective_id=0, has_side_effects=True, vmem_limit_bytes=40 << 20
        ),
        name="brick",
    )(
        *(pinned(x) for x in (fraction, velocity, centres)), counts,
        *(pinned(x) for x in (points, active_points, rigid_start, mass.reshape(1, 128), inertia.reshape(1, 128))),
    )
    return pl.pallas_call(
        pass_kernel,
        out_shape=outs,
        in_specs=[anywhere] * 4,
        out_specs=(hbm,) * 4,
        scratch_shapes=[pltpu.SemaphoreType.DMA((4,))],
        compiler_params=pltpu.CompilerParams(vmem_limit_bytes=4 << 20),
        name="pass_on",
    )(*results)


def solution(mesh):
    bricks = ("gx", "gy", "gz")
    placed = (
        P("gz", "gx", "gy"), P(None, "gz", "gx", "gy"), P(None, bricks), P(bricks, None), P(bricks, None),
        P(bricks), P(None, bricks), P(bricks), P(bricks),
    )
    return jax.shard_map(
        body, mesh=mesh, in_specs=placed,
        out_specs=(P("gz", "gx", "gy"), P("gx", "gy"), P(None, bricks, None), P(None, bricks)),
        check_vma=False,
    )
```
